256 devices in a mesh: shot: 16 (over y, z_lo, core), dom: 16 (over z_hi, x).
Axes of the slice: x: 4, y: 4, z: 8 (z_hi: 4, z_lo: 2; z = z_hi * 2 + z_lo), core: 2. Of those that a mesh axis runs over, the one named last changes fastest.
Arguments:
- velocity_term: float32 [128, 8, 2048], P('dom'), may hold values from 0.05 to 0.3
- wave_prev: float32 [64, 128, 8, 2048], P('shot', 'dom'), may hold values from -6 to 6
- wave_now: float32 [64, 128, 8, 2048], P('shot', 'dom'), may hold values from -6 to 6
- adjoint_next: float32 [64, 128, 8, 2048], P('shot', 'dom'), may hold values from -6 to 6
- adjoint_now: float32 [64, 128, 8, 2048], P('shot', 'dom'), may hold values from -6 to 6
- source_cell: int32 [64], P('shot'), may hold values from 0 to 2097151
- source_wave: float32 [64, 2], P('shot'), may hold values from -16 to 16
- receiver_cells: int32 [64, 256], P('shot'), may hold values from 0 to 2097151
- data_residual: float32 [64, 2, 256], P('shot'), may hold values from -6 to 6
- aperture: int32 [64, 8], P('shot'), may hold values from 0 to 15, all different within a row
Outputs:
- gradient: float32 [128, 8, 2048], P('dom')
The draws below stay inside these ranges and needn't reach their ends.
Inputs may be any that keep to these rules, and one draw needn't show every extreme that they name: `aperture`: each row names 8 different domain blocks, and every block is named by some shot.
All inputs are finite; a program needn't handle non-finite values.
Results may differ from the reference program's by a relative error of at most 0.0003.
Values sent between devices are 32-bit elements; how exact they have to be, the bound alone decides.
A program may use at most 128 MiB of HBM per device.

```python
import math
import jax
import jax.numpy as jnp
from jax import lax

CX = 8
LEV = 8
NY = 2048
NREC = 256
NX = 128
SHOTS = 64
APER = 8
N_DOM = 16


def touch_ends(drawn, key, least, high):
    extent = drawn.shape
    spot = [jax.random.randint(jax.random.fold_in(key, axis), (), 0, extent[axis]) for axis in range(len(extent))]
    drawn = drawn.at[tuple(spot)].set(least)
    longest = extent.index(max(extent))
    spot[longest] = (spot[longest] + 1) % extent[longest]
    return drawn.at[tuple(spot)].set(high)


def levels(rng, dims, pieces, least, high):
    def one(position, shards_of):
        steps = jax.random.uniform(jax.random.fold_in(jax.random.fold_in(rng, 6), position), (shards_of,), jnp.float32, least / len(pieces), high / len(pieces))
        return jnp.repeat(jnp.exp(steps), dims[position] // shards_of).reshape((-1,) + (1,) * (len(dims) - position - 1))

    loudness = one(*pieces[0])
    for cut in pieces[1:]:
        loudness = loudness * one(*cut)
    return loudness


def different_ones(key, rows, number_of, top, lift):
    order = jax.random.permutation(jax.random.fold_in(key, 1), number_of)
    pull = order
    for power in range(3):
        pull = pull * pull // number_of
    pull = pull * lift // number_of
    tickets = jax.random.randint(jax.random.fold_in(key, 2), (rows, number_of), 0, 4096) + pull
    fixed_rows = jax.random.permutation(jax.random.fold_in(key, 3), rows)[jnp.arange(number_of) % rows]
    tickets = jnp.where(jnp.arange(rows)[:, None] == fixed_rows[None, :], 1 << 14, tickets)
    merit = tickets * number_of + jnp.arange(number_of)
    return lax.top_k(merit.astype(jnp.int32), top)[1].astype(jnp.int32)


def bell_draw(key, dims, deviation, bound, cuts=(), kind=jnp.bfloat16):
    gain = levels(key, dims, cuts, -0.22, 0.18) if cuts else 1.0
    values = jax.random.normal(key, dims, jnp.float32) * deviation * gain
    return jnp.minimum(jnp.maximum(values, -bound), bound).astype(kind)


def setup_inputs(seed: int = 0) -> dict:
    splits = jax.random.split(jax.random.key(seed), 11)
    velocity_term = jnp.clip(jnp.exp(math.log(0.3) - 1.7917595 * jax.random.uniform(splits[0], (NX, LEV, NY), jnp.float32) ** levels(splits[0], (NX, LEV, NY), ((0, 16),), -0.2, 0.2)), 0.05, 0.3)
    wave_prev = bell_draw(splits[1], (SHOTS, NX, LEV, NY), 1.0, 6.0, ((0, 16), (1, 16)), jnp.float32)
    wave_now = bell_draw(splits[2], (SHOTS, NX, LEV, NY), 1.0, 6.0, ((0, 16), (1, 16)), jnp.float32)
    adjoint_next = bell_draw(splits[3], (SHOTS, NX, LEV, NY), 1.0, 6.0, ((0, 16), (1, 16)), jnp.float32)
    adjoint_now = bell_draw(splits[4], (SHOTS, NX, LEV, NY), 1.0, 6.0, ((0, 16), (1, 16)), jnp.float32)
    source_cell = touch_ends(jax.random.randint(splits[5], (SHOTS,), 0, NX * LEV * NY), jax.random.fold_in(splits[5], 1), 0, (NX * LEV * NY) - 1).astype(jnp.int32)
    source_wave = bell_draw(splits[6], (SHOTS, 2), 4.0, 16.0, ((0, 16),), jnp.float32)
    receiver_cells = touch_ends(jax.random.randint(splits[7], (SHOTS, NREC), 0, NX * LEV * NY), jax.random.fold_in(splits[7], 1), 0, (NX * LEV * NY) - 1).astype(jnp.int32)
    data_residual = bell_draw(splits[8], (SHOTS, 2, NREC), 1.0, 6.0, ((0, 16),), jnp.float32)
    aperture = different_ones(splits[9], SHOTS, N_DOM, APER, 4096)
    return {"velocity_term": velocity_term, "wave_prev": wave_prev, "wave_now": wave_now, "adjoint_next": adjoint_next, "adjoint_now": adjoint_now, "source_cell": source_cell, "source_wave": source_wave, "receiver_cells": receiver_cells, "data_residual": data_residual, "aperture": aperture}


def laplace(field):
    padded = jnp.pad(field, 1)
    beside = padded[2:, 1:-1, 1:-1] + padded[:-2, 1:-1, 1:-1]
    beside = beside + padded[1:-1, 2:, 1:-1] + padded[1:-1, :-2, 1:-1]
    beside = beside + padded[1:-1, 1:-1, 2:] + padded[1:-1, 1:-1, :-2]
    return beside - 6.0 * field


def inject(field, cells, values):
    flat = field.reshape(-1).at[cells].add(values)
    return flat.reshape(field.shape)


def reference(velocity_term, wave_prev, wave_now, adjoint_next, adjoint_now, source_cell, source_wave, receiver_cells, data_residual, aperture):
    blocks = jnp.arange(NX, dtype=jnp.int32) // CX

    def one_shot(total, inputs):
        before, now, after, adjoint, cell, wavelet, cells, misfit, chosen = inputs
        wave_one = 2.0 * now - before + velocity_term * laplace(now)
        wave_one = inject(wave_one, cell.reshape(1), wavelet[0].reshape(1))
        wave_two = 2.0 * wave_one - now + velocity_term * laplace(wave_one)
        wave_two = inject(wave_two, cell.reshape(1), wavelet[1].reshape(1))
        adjoint_one = 2.0 * adjoint - after + velocity_term * laplace(adjoint)
        adjoint_one = inject(adjoint_one, cells, misfit[0])
        adjoint_zero = 2.0 * adjoint_one - adjoint + velocity_term * laplace(adjoint_one)
        adjoint_zero = inject(adjoint_zero, cells, misfit[1])
        image = adjoint_one * (wave_two - 2.0 * wave_one + now) + adjoint_zero * (wave_one - 2.0 * now + before)
        inside = jnp.any(blocks[:, None] == chosen[None, :], axis=1).astype(jnp.float32)
        return total + image * inside[:, None, None], None

    start = jnp.zeros((NX, LEV, NY), jnp.float32)
    total, unused = lax.scan(one_shot, start, (wave_prev, wave_now, adjoint_next, adjoint_now, source_cell, source_wave, receiver_cells, data_residual, aperture))
    return total * (float(SHOTS) ** -0.5)
```

```python
import functools

import jax
import jax.numpy as jnp
from jax import lax
from jax.experimental import pallas as pl
from jax.experimental.pallas import tpu as pltpu
from jax.sharding import PartitionSpec as P

MESH = pl.DeviceIdType.MESH
SHOTS = 4
PLANES = 8
LEVELS = 8
COLUMNS = 2048
LANES = 128
TILES = COLUMNS // LANES
RECEIVERS = 256
GROUP = 16
HALF = COLUMNS // 2
CELLS = PLANES * LEVELS * COLUMNS
EIGHTH = COLUMNS // 8
UP, DOWN = 0, 1
ENDS = (PLANES, 1)
GHOSTS = (0, PLANES + 1)


def kernel(
    scale,
    vel_hbm,
    wave_prev_hbm,
    wave_now_hbm,
    adj_next_hbm,
    adj_now_hbm,
    source_cell,
    source_wave,
    cells_ref,
    residual_ref,
    aperture,
    out_ref,
    vel,
    wave0,
    wave1,
    adj0,
    adj1,
    prev,
    after,
    injected,
    inner,
    edge,
    edge_out,
    relay_buf,
    inner_got,
    inner_part,
    pair_got,
    edge_got,
    load_sem,
    vel_sem,
    send_sem,
    recv_sem,
    relay_send,
    relay_recv,
    red_send,
    red_recv,
    pair_sem,
    gather_send,
    gather_recv,
    edge_send,
    edge_recv,
    spread_send,
    spread_recv,
):
    shot = lax.axis_index("shot")
    dom = lax.axis_index("dom")
    column = lax.rem(dom, 4)
    row = dom // 4
    lower = lax.rem(shot // 2, 2)
    eighth = (shot // 4) * 2 + lax.rem(shot, 2)

    def along_dom(step):
        return {"dom": lax.rem(dom + step + GROUP, GROUP)}

    def member(index):
        return {"shot": (index // 2) * 4 + lower * 2 + lax.rem(index, 2)}

    towards = (along_dom(1), along_dom(-1))
    has = (dom < GROUP - 1, dom > 0)
    from_has = (dom > 0, dom < GROUP - 1)
    crosses = (column == 3, column == 0)
    from_crosses = (column == 0, column == 3)
    relays = ((column == 0) & (row < 3), (column == 3) & (row > 0))
    relay_first = (along_dom(-3), along_dom(3))
    relay_second = (along_dom(4), along_dom(-4))

    def load(s):
        return [
            pltpu.make_async_copy(source.at[s], target, load_sem.at[s, k])
            for k, (source, target) in enumerate(
                (
                    (wave_now_hbm, wave0.at[s, pl.ds(1, PLANES)]),
                    (adj_now_hbm, adj0.at[s, pl.ds(1, PLANES)]),
                    (wave_prev_hbm, prev.at[s]),
                    (adj_next_hbm, after.at[s]),
                )
            )
        ]

    vel_load = pltpu.make_async_copy(vel_hbm, vel, vel_sem)
    vel_load.start()
    for s in range(SHOTS):
        for copy in load(s):
            copy.start()

    barrier = pltpu.get_barrier_semaphore()

    def greet(device):
        pl.semaphore_signal(barrier, inc=1, device_id=device, device_id_type=MESH)

    def greet_peer(k, carry):
        greet({"shot": lax.rem(shot + k, GROUP)})
        return carry

    lax.fori_loop(1, GROUP, greet_peer, 0)
    greet(towards[UP])
    greet(towards[DOWN])

    @pl.when(column == 0)
    def _():
        greet(along_dom(3))
        greet(along_dom(4))
        greet(along_dom(-4))

    @pl.when(column == 3)
    def _():
        greet(along_dom(-3))
        greet(along_dom(4))
        greet(along_dom(-4))

    relaying = (column == 0) | (column == 3)
    pl.semaphore_wait(barrier, GROUP + 1 + jnp.where(relaying, 3, 0))

    blocks = ((wave0, adj0), (wave1, adj1))

    def layer_refs(step, field, s, way):
        block = blocks[step][field]
        if step == 0:
            source = (wave_now_hbm, adj_now_hbm)[field].at[s, ENDS[way] - 1]
        else:
            source = block.at[s, ENDS[way]]
        return source, block.at[s, GHOSTS[way]]

    def remote(source, target, send, recv, device):
        return pltpu.make_async_remote_copy(
            src_ref=source,
            dst_ref=target,
            send_sem=send,
            recv_sem=recv,
            device_id=device,
            device_id_type=MESH,
        )

    first_half, second_half = pl.ds(0, HALF), pl.ds(HALF, HALF)

    def whole(step, field, s, way):
        source, target = layer_refs(step, field, s, way)
        k = 2 * step + field
        return remote(source, target, send_sem.at[way, k, s], recv_sem.at[way, k, s], towards[way])

    def direct(step, field, s, way):
        source, target = layer_refs(step, field, s, way)
        k = 2 * step + field
        return remote(
            source.at[:, first_half],
            target.at[:, first_half],
            send_sem.at[way, k, s],
            recv_sem.at[way, k, s],
            towards[way],
        )

    def leg_one(step, field, s, way):
        source, _ = layer_refs(step, field, s, way)
        k = 2 * step + field
        return remote(
            source.at[:, second_half],
            relay_buf.at[k, s],
            relay_send.at[0, k, s],
            relay_recv.at[0, k, s],
            relay_first[way],
        )

    def leg_two(step, field, s, way):
        _, target = layer_refs(step, field, s, way)
        k = 2 * step + field
        return remote(
            relay_buf.at[k, s],
            target.at[:, second_half],
            relay_send.at[1, k, s],
            relay_recv.at[1, k, s],
            relay_second[way],
        )

    def send_layers(step, s):
        for field in (0, 1):
            for way in (UP, DOWN):

                @pl.when(has[way] & crosses[way])
                def _():
                    leg_one(step, field, s, way).start()
                    direct(step, field, s, way).start()

                @pl.when(has[way] & jnp.logical_not(crosses[way]))
                def _():
                    whole(step, field, s, way).start()

    def pass_on(step, s):
        for field in (0, 1):
            for way in (UP, DOWN):

                @pl.when(relays[way])
                def _():
                    leg_one(step, field, s, way).wait_recv()
                    leg_two(step, field, s, way).start()

    def take_layers(step, s):
        for field in (0, 1):
            for way in (UP, DOWN):

                @pl.when(from_has[way] & from_crosses[way])
                def _():
                    direct(step, field, s, way).wait_recv()
                    leg_two(step, field, s, way).wait_recv()

                @pl.when(from_has[way] & jnp.logical_not(from_crosses[way]))
                def _():
                    whole(step, field, s, way).wait_recv()

    def end_sends(step, s):
        for field in (0, 1):
            for way in (UP, DOWN):

                @pl.when(has[way] & crosses[way])
                def _():
                    leg_one(step, field, s, way).wait_send()
                    direct(step, field, s, way).wait_send()

                @pl.when(has[way] & jnp.logical_not(crosses[way]))
                def _():
                    whole(step, field, s, way).wait_send()

                @pl.when(relays[way])
                def _():
                    leg_two(step, field, s, way).wait_send()

    def each_shot(body):
        def step(s, carry):
            body(s)
            return carry

        lax.fori_loop(0, SHOTS, step, 0)

    each_shot(lambda s: send_layers(0, s))

    for way in (UP, DOWN):

        @pl.when(jnp.logical_not(from_has[way]))
        def _():
            def clear(s):
                nothing = jnp.zeros((LEVELS, COLUMNS), jnp.float32)
                for block in (wave0, adj0, wave1, adj1):
                    block[s, GHOSTS[way]] = nothing

            each_shot(clear)

    level = lax.broadcasted_iota(jnp.int32, (LEVELS, LANES), 0)
    lane = lax.broadcasted_iota(jnp.int32, (LEVELS, LANES), 1)
    place = level * LANES + lane
    top, bottom = level == 0, level == LEVELS - 1
    leftmost, rightmost = lane == 0, lane == LANES - 1

    def columns_of(t):
        return pl.ds(t * LANES, LANES)

    def laplace(ref, s, x):
        empty = jnp.zeros((LEVELS, LANES), jnp.float32)
        here = ref[s, x, :, columns_of(0)]
        right_of = pltpu.roll(here, LANES - 1, 1)
        before = empty
        for t in range(TILES):
            if t + 1 < TILES:
                following = ref[s, x, :, columns_of(t + 1)]
                right_next = pltpu.roll(following, LANES - 1, 1)
            else:
                following, right_next = empty, empty
            shifted = pltpu.roll(here, 1, 1)
            left = jnp.where(leftmost, before, shifted)
            right = jnp.where(rightmost, right_next, right_of)
            above = jnp.where(top, 0.0, pltpu.roll(here, 1, 0))
            below = jnp.where(bottom, 0.0, pltpu.roll(here, LEVELS - 1, 0))
            beside = ref[s, x - 1, :, columns_of(t)] + ref[s, x + 1, :, columns_of(t)]
            beside = (beside + (above + below)) + (left + right)
            yield here, beside - 6.0 * here
            before, here, right_of = shifted, following, right_next

    def source_of(s):
        local = source_cell[s] - dom * CELLS
        tile = (local >> 14) * TILES + ((local >> 7) & (TILES - 1))
        return (tile * LEVELS + ((local >> 11) & (LEVELS - 1))) * LANES + (local & (LANES - 1))

    def rows_of(x, t):
        return pl.ds(pl.multiple_of(((x - 1) * TILES + t) * LEVELS, LEVELS), LEVELS)

    def first_step(s, x):
        at = source_of(s) - (x - 1) * (TILES * LEVELS * LANES)
        wavelet = source_wave[s, 0]
        both = zip(laplace(wave0, s, x), laplace(adj0, s, x), strict=True)
        for t, ((wave, wave_lap), (adj, adj_lap)) in enumerate(both):
            cols = columns_of(t)
            v = vel[x - 1, :, cols]
            pushed = v * wave_lap + jnp.where(place == at - t * (LEVELS * LANES), wavelet, 0.0)
            wave1[s, x, :, cols] = (2.0 * wave - prev[s, x - 1, :, cols]) + pushed
            prev[s, x - 1, :, cols] = pushed
            drawn = injected[s, rows_of(x, t), pl.ds(0, LANES)]
            adj1[s, x, :, cols] = (2.0 * adj - after[s, x - 1, :, cols]) + (v * adj_lap + drawn)

    def second_step(s, x, total, place_x, first):
        at = source_of(s) - (x - 1) * (TILES * LEVELS * LANES)
        wavelet = source_wave[s, 1]
        inside = aperture[s, 0] == dom
        for k in range(1, 8):
            inside = inside | (aperture[s, k] == dom)
        weight = jnp.where(inside, scale, 0.0)
        both = zip(laplace(wave1, s, x), laplace(adj1, s, x), strict=True)
        for t, ((_, wave_lap), (adj, adj_lap)) in enumerate(both):
            cols = columns_of(t)
            v = vel[x - 1, :, cols]
            pushed = v * wave_lap + jnp.where(place == at - t * (LEVELS * LANES), wavelet, 0.0)
            drawn = injected[s, rows_of(x, t), pl.ds(LANES, LANES)]
            zero = (2.0 * adj - adj0[s, x, :, cols]) + (v * adj_lap + drawn)
            image = weight * (adj * pushed + zero * prev[s, x - 1, :, cols])
            total[place_x, :, cols] = image if first else total[place_x, :, cols] + image

    def inject(s):
        local = cells_ref[pl.ds(s, 1), :] - dom * CELLS
        tile = (local >> 14) * TILES + ((local >> 7) & (TILES - 1))
        line = tile * LEVELS + ((local >> 11) & (LEVELS - 1))
        spot = local & (LANES - 1)
        lines = PLANES * TILES * LEVELS
        picks = lax.broadcasted_iota(jnp.int32, (lines, RECEIVERS), 0) == line
        picks = jnp.where(picks, 1.0, 0.0).astype(jnp.bfloat16)
        hits = lax.broadcasted_iota(jnp.int32, (LANES, RECEIVERS), 0) == spot
        parts = []
        for step in (0, 1):
            rest = residual_ref[s, pl.ds(step, 1), :]
            pieces = []
            for _ in range(3):
                piece = rest.astype(jnp.bfloat16).astype(jnp.float32)
                rest = rest - piece
                pieces.append(jnp.where(hits, piece, 0.0).astype(jnp.bfloat16))
            parts.append(jnp.concatenate(pieces, axis=1))
        injected[s] = lax.dot_general(
            jnp.concatenate([picks] * 3, axis=1),
            jnp.concatenate(parts, axis=0),
            (((1,), (1,)), ((), ())),
            preferred_element_type=jnp.float32,
        )

    def planes(first, last, body):
        def step(x, carry):
            body(x)
            return carry

        lax.fori_loop(first, last, step, 0)

    vel_load.wait()

    def inner_first(s):
        inject(s)
        for copy in load(s):
            copy.wait()
        planes(2, PLANES, lambda x: first_step(s, x))

    each_shot(inner_first)

    def clear_inner(x):
        inner[x] = jnp.zeros((LEVELS, COLUMNS), jnp.float32)

    planes(0, PLANES - 2, clear_inner)

    def ends_first(s):
        pass_on(0, s)
        take_layers(0, s)
        planes(0, 2, lambda k: first_step(s, 1 + k * (PLANES - 1)))
        send_layers(1, s)
        planes(2, PLANES, lambda x: second_step(s, x, inner, x - 2, False))

    each_shot(ends_first)

    def eighth_of(index):
        return pl.ds(pl.multiple_of(index * EIGHTH, EIGHTH), EIGHTH)

    def scatter(k):
        peer = lax.rem(eighth + k, 8)
        return remote(
            inner.at[:, :, eighth_of(peer)],
            inner_got.at[k],
            red_send.at[k],
            red_recv.at[k],
            member(peer),
        )

    def gather(k):
        mine = out_ref.at[pl.ds(1, PLANES - 2), :, eighth_of(eighth)]
        return remote(
            mine, mine, gather_send.at[k], gather_recv.at[k], member(lax.rem(eighth + k, 8))
        )

    def gathered(k):
        peer = lax.rem(eighth - k + 8, 8)
        there = out_ref.at[pl.ds(1, PLANES - 2), :, eighth_of(peer)]
        return remote(there, there, gather_send.at[k], gather_recv.at[k], member(peer))

    def every(count, body):
        def step(k, carry):
            body(k)
            return carry

        lax.fori_loop(1, count, step, 0)

    every(8, lambda k: scatter(k).start())

    def clear_edge(x):
        edge[x] = jnp.zeros((LEVELS, COLUMNS), jnp.float32)

    planes(0, 2, clear_edge)

    def ends_second(s):
        pass_on(1, s)
        take_layers(1, s)
        planes(0, 2, lambda k: second_step(s, 1 + k * (PLANES - 1), edge, k, False))

    ends_second(0)

    inner_part[...] = inner[:, :, eighth_of(eighth)]

    def add_inner(k):
        scatter(k).wait_recv()
        inner_part[...] += inner_got[k]

    every(8, add_inner)
    swap = remote(
        inner_part,
        pair_got,
        pair_sem.at[0],
        pair_sem.at[1],
        {"shot": shot + 2 - 4 * lower},
    )
    swap.start()

    ends_second(1)

    swap.wait_recv()
    out_ref[pl.ds(1, PLANES - 2), :, eighth_of(eighth)] = inner_part[...] + pair_got[...]
    every(8, lambda k: gather(k).start())

    ends_second(2)
    ends_second(3)

    def lane_tile(index):
        return pl.ds(pl.multiple_of(index * LANES, LANES), LANES)

    def scatter_edge(k):
        peer = lax.rem(shot + k, GROUP)
        return remote(
            edge.at[:, :, lane_tile(peer)],
            edge_got.at[k],
            edge_send.at[k],
            edge_recv.at[k],
            {"shot": peer},
        )

    def spread(k):
        mine = edge_out.at[:, :, lane_tile(shot)]
        return remote(
            mine, mine, spread_send.at[k], spread_recv.at[k], {"shot": lax.rem(shot + k, GROUP)}
        )

    def spread_from(k):
        peer = lax.rem(shot - k + GROUP, GROUP)
        there = edge_out.at[:, :, lane_tile(peer)]
        return remote(there, there, spread_send.at[k], spread_recv.at[k], {"shot": peer})

    every(GROUP, lambda k: scatter_edge(k).start())

    def add_edge(k, carry):
        scatter_edge(k).wait_recv()
        return carry + edge_got[k]

    edge_out[:, :, lane_tile(shot)] = lax.fori_loop(1, GROUP, add_edge, edge[:, :, lane_tile(shot)])
    every(GROUP, lambda k: spread(k).start())

    for step in (0, 1):
        each_shot(functools.partial(end_sends, step))
    swap.wait_send()
    every(8, lambda k: scatter(k).wait_send())
    every(8, lambda k: gather(k).wait_send())
    every(8, lambda k: gathered(k).wait_recv())
    every(GROUP, lambda k: scatter_edge(k).wait_send())
    every(GROUP, lambda k: spread(k).wait_send())
    every(GROUP, lambda k: spread_from(k).wait_recv())
    out_ref[0] = edge_out[0]
    out_ref[PLANES - 1] = edge_out[1]


def body(*arguments):
    scale = float(lax.axis_size("shot") * SHOTS) ** (-0.5)
    f32 = jnp.float32
    block = (LEVELS, COLUMNS)
    dma = pltpu.SemaphoreType.DMA
    hbm = pl.BlockSpec(memory_space=pltpu.HBM)
    vmem = pl.BlockSpec(memory_space=pltpu.VMEM)
    smem = pl.BlockSpec(memory_space=pltpu.SMEM)
    return pl.pallas_call(
        functools.partial(kernel, scale),
        out_shape=jax.ShapeDtypeStruct((PLANES, *block), f32),
        in_specs=[hbm, hbm, hbm, hbm, hbm, smem, smem, vmem, vmem, smem],
        out_specs=vmem,
        scratch_shapes=[
            pltpu.VMEM((PLANES, *block), f32),
            pltpu.VMEM((SHOTS, PLANES + 2, *block), f32),
            pltpu.VMEM((SHOTS, PLANES + 2, *block), f32),
            pltpu.VMEM((SHOTS, PLANES + 2, *block), f32),
            pltpu.VMEM((SHOTS, PLANES + 2, *block), f32),
            pltpu.VMEM((SHOTS, PLANES, *block), f32),
            pltpu.VMEM((SHOTS, PLANES, *block), f32),
            pltpu.VMEM((SHOTS, CELLS // LANES, 2 * LANES), f32),
            pltpu.VMEM((PLANES - 2, *block), f32),
            pltpu.VMEM((2, *block), f32),
            pltpu.VMEM((2, *block), f32),
            pltpu.VMEM((4, SHOTS, LEVELS, HALF), f32),
            pltpu.VMEM((8, PLANES - 2, LEVELS, EIGHTH), f32),
            pltpu.VMEM((PLANES - 2, LEVELS, EIGHTH), f32),
            pltpu.VMEM((PLANES - 2, LEVELS, EIGHTH), f32),
            pltpu.VMEM((GROUP, 2, LEVELS, LANES), f32),
            dma((SHOTS, 4)),
            dma,
            dma((2, 4, SHOTS)),
            dma((2, 4, SHOTS)),
            dma((2, 4, SHOTS)),
            dma((2, 4, SHOTS)),
            dma((8,)),
            dma((8,)),
            dma((2,)),
            dma((8,)),
            dma((8,)),
            dma((GROUP,)),
            dma((GROUP,)),
            dma((GROUP,)),
            dma((GROUP,)),
        ],
        compiler_params=pltpu.CompilerParams(
            collective_id=0, has_side_effects=True, vmem_limit_bytes=48 * 2**20
        ),
        name="gradient",
    )(*arguments)


def solution(mesh):
    placed = (
        P("dom", None, None),
        P("shot", "dom", None, None),
        P("shot", "dom", None, None),
        P("shot", "dom", None, None),
        P("shot", "dom", None, None),
        P("shot"),
        P("shot", None),
        P("shot", None),
        P("shot", None, None),
        P("shot", None),
    )
    return jax.shard_map(
        body, mesh=mesh, in_specs=placed, out_specs=P("dom", None, None), check_vma=False
    )
```

```python
import functools

import jax
import jax.numpy as jnp
from jax import lax
from jax.experimental import pallas as pl
from jax.experimental.pallas import tpu as pltpu
from jax.sharding import PartitionSpec as P

MESH = pl.DeviceIdType.MESH
SHOTS = 4
PLANES = 8
LEVELS = 8
COLUMNS = 2048
LANES = 128
TILES = COLUMNS // LANES
RECEIVERS = 256
GROUP = 16
HALF = COLUMNS // 2
CELLS = PLANES * LEVELS * COLUMNS
EIGHTH = COLUMNS // 8
UP, DOWN = 0, 1
ENDS = (PLANES, 1)
GHOSTS = (0, PLANES + 1)


def kernel(
    scale,
    vel_hbm,
    wave_prev_hbm,
    wave_now_hbm,
    adj_next_hbm,
    adj_now_hbm,
    source_cell_hbm,
    source_wave_hbm,
    cells_hbm,
    residual_hbm,
    aperture_hbm,
    out_ref,
    source_cell,
    source_wave,
    cells_ref,
    residual_ref,
    aperture,
    vel,
    wave0,
    wave1,
    adj0,
    adj1,
    prev,
    after,
    injected,
    inner,
    edge,
    edge_out,
    ends,
    vel_ghost,
    relay_buf,
    inner_got,
    inner_part,
    pair_got,
    edge_got,
    load_sem,
    small_sem,
    vel_send,
    vel_recv,
    send_sem,
    recv_sem,
    relay_send,
    relay_recv,
    red_send,
    red_recv,
    pair_sem,
    gather_send,
    gather_recv,
    edge_send,
    edge_recv,
    spread_send,
    spread_recv,
):
    shot = lax.axis_index("shot")
    dom = lax.axis_index("dom")
    column = lax.rem(dom, 4)
    row = dom // 4
    lower = lax.rem(shot // 2, 2)
    eighth = (shot // 4) * 2 + lax.rem(shot, 2)

    def along_dom(step):
        return {"dom": lax.rem(dom + step + GROUP, GROUP)}

    def member(index):
        return {"shot": (index // 2) * 4 + lower * 2 + lax.rem(index, 2)}

    towards = (along_dom(1), along_dom(-1))
    has = (dom < GROUP - 1, dom > 0)
    from_has = (dom > 0, dom < GROUP - 1)
    crosses = (column == 3, column == 0)
    from_crosses = (column == 0, column == 3)
    relays = ((column == 0) & (row < 3), (column == 3) & (row > 0))
    relay_first = (along_dom(-3), along_dom(3))
    relay_second = (along_dom(4), along_dom(-4))

    def load(s):
        return [
            pltpu.make_async_copy(source.at[s], target, load_sem.at[s, k])
            for k, (source, target) in enumerate(
                (
                    (wave_now_hbm, wave0.at[s, pl.ds(1, PLANES)]),
                    (adj_now_hbm, adj0.at[s, pl.ds(1, PLANES)]),
                    (wave_prev_hbm, prev.at[s]),
                    (adj_next_hbm, after.at[s]),
                )
            )
        ]

    small_loads = [
        pltpu.make_async_copy(source, target, small_sem.at[k])
        for k, (source, target) in enumerate(
            (
                (cells_hbm, cells_ref),
                (residual_hbm, residual_ref),
                (vel_hbm, vel),
                (source_cell_hbm, source_cell),
                (source_wave_hbm, source_wave),
                (aperture_hbm, aperture),
            )
        )
    ]
    for copy in small_loads:
        copy.start()
    for s in range(SHOTS):
        for copy in load(s):
            copy.start()

    barrier = pltpu.get_barrier_semaphore()

    def greet(device):
        pl.semaphore_signal(barrier, inc=1, device_id=device, device_id_type=MESH)

    def greet_peer(k, carry):
        greet({"shot": lax.rem(shot + k, GROUP)})
        return carry

    lax.fori_loop(1, GROUP, greet_peer, 0)
    greet(towards[UP])
    greet(towards[DOWN])

    @pl.when(column == 0)
    def _():
        greet(along_dom(3))
        greet(along_dom(4))
        greet(along_dom(-4))

    @pl.when(column == 3)
    def _():
        greet(along_dom(-3))
        greet(along_dom(4))
        greet(along_dom(-4))

    relaying = (column == 0) | (column == 3)
    pl.semaphore_wait(barrier, GROUP + 1 + jnp.where(relaying, 3, 0))

    fields = ((wave_now_hbm, wave0), (adj_now_hbm, adj0), (None, wave1), (None, adj1))

    def layer_refs(k, s, way):
        given, block = fields[k]
        source = ends.at[way, k - 2, s] if given is None else given.at[s, ENDS[way] - 1]
        return source, block.at[s, GHOSTS[way]]

    def remote(source, target, send, recv, device):
        return pltpu.make_async_remote_copy(
            src_ref=source,
            dst_ref=target,
            send_sem=send,
            recv_sem=recv,
            device_id=device,
            device_id_type=MESH,
        )

    first_half, second_half = pl.ds(0, HALF), pl.ds(HALF, HALF)

    def whole(k, s, way):
        source, target = layer_refs(k, s, way)
        return remote(source, target, send_sem.at[way, k, s], recv_sem.at[way, k, s], towards[way])

    def direct(k, s, way):
        source, target = layer_refs(k, s, way)
        return remote(
            source.at[:, first_half],
            target.at[:, first_half],
            send_sem.at[way, k, s],
            recv_sem.at[way, k, s],
            towards[way],
        )

    def leg_one(k, s, way):
        source, _ = layer_refs(k, s, way)
        return remote(
            source.at[:, second_half],
            relay_buf.at[k, s],
            relay_send.at[0, k, s],
            relay_recv.at[0, k, s],
            relay_first[way],
        )

    def leg_two(k, s, way):
        _, target = layer_refs(k, s, way)
        return remote(
            relay_buf.at[k, s],
            target.at[:, second_half],
            relay_send.at[1, k, s],
            relay_recv.at[1, k, s],
            relay_second[way],
        )

    def when_each(conditions, body):
        for way in (UP, DOWN):
            pl.when(conditions[way])(functools.partial(body, way))

    def both(one, other):
        return tuple(a & b for a, b in zip(one, other, strict=True))

    def but(one, other):
        return tuple(a & jnp.logical_not(b) for a, b in zip(one, other, strict=True))

    far, near = both(has, crosses), but(has, crosses)
    from_far, from_near = both(from_has, from_crosses), but(from_has, from_crosses)

    def send_first_legs(k, s):
        when_each(far, lambda way: leg_one(k, s, way).start())

    def send_layer(k, s):
        when_each(far, lambda way: direct(k, s, way).start())
        when_each(near, lambda way: whole(k, s, way).start())

    def advance(k, s):
        when_each(far, lambda way: direct(k, s, way).wait_send())
        when_each(near, lambda way: whole(k, s, way).wait_send())
        pl.when(s < SHOTS - 2)(lambda: send_layer(k, s + 2))
        if k < 3:
            pl.when(s >= SHOTS - 2)(lambda: send_layer(k + 1, s + 2 - SHOTS))

        def pass_on(way):
            leg_one(k, s, way).wait_recv()
            leg_two(k, s, way).start()

        when_each(relays, pass_on)

    def take_layer(k, s):
        def two_halves(way):
            direct(k, s, way).wait_recv()
            leg_two(k, s, way).wait_recv()

        when_each(from_far, two_halves)
        when_each(from_near, lambda way: whole(k, s, way).wait_recv())

    def end_legs(k, s):
        when_each(far, lambda way: leg_one(k, s, way).wait_send())
        when_each(relays, lambda way: leg_two(k, s, way).wait_send())

    def vel_layer(way):
        return remote(
            vel_hbm.at[ENDS[way] - 1],
            vel_ghost.at[way],
            vel_send.at[way],
            vel_recv.at[way],
            towards[way],
        )

    def each_shot(body):
        def step(s, carry):
            body(s)
            return carry

        lax.fori_loop(0, SHOTS, step, 0)

    for k in (0, 1):
        each_shot(functools.partial(send_first_legs, k))
    when_each(has, lambda way: vel_layer(way).start())
    send_layer(0, 0)
    send_layer(0, 1)

    def clear_ghosts(way):
        nothing = jnp.zeros((LEVELS, COLUMNS), jnp.float32)
        vel_ghost[way] = nothing

        def clear(s):
            for block in (wave0, adj0, wave1, adj1):
                block[s, GHOSTS[way]] = nothing

        each_shot(clear)

    when_each(tuple(jnp.logical_not(there) for there in from_has), clear_ghosts)

    level = lax.broadcasted_iota(jnp.int32, (LEVELS, LANES), 0)
    lane = lax.broadcasted_iota(jnp.int32, (LEVELS, LANES), 1)
    place = level * LANES + lane
    top, bottom = level == 0, level == LEVELS - 1
    leftmost, rightmost = lane == 0, lane == LANES - 1

    def columns_of(t):
        return pl.ds(t * LANES, LANES)

    def laplace(ref, s, x, sides=None):
        sides = (x - 1, x + 1) if sides is None else sides
        empty = jnp.zeros((LEVELS, LANES), jnp.float32)
        here = ref[s, x, :, columns_of(0)]
        right_of = pltpu.roll(here, LANES - 1, 1)
        before = empty
        for t in range(TILES):
            if t + 1 < TILES:
                following = ref[s, x, :, columns_of(t + 1)]
                right_next = pltpu.roll(following, LANES - 1, 1)
            else:
                following, right_next = empty, empty
            shifted = pltpu.roll(here, 1, 1)
            left = jnp.where(leftmost, before, shifted)
            right = jnp.where(rightmost, right_next, right_of)
            above = jnp.where(top, 0.0, pltpu.roll(here, 1, 0))
            below = jnp.where(bottom, 0.0, pltpu.roll(here, LEVELS - 1, 0))
            beside = (above + below) + (left + right)
            for side in sides:
                beside = beside + ref[s, side, :, columns_of(t)]
            yield here, beside - 6.0 * here
            before, here, right_of = shifted, following, right_next

    def source_of(s):
        local = source_cell[s] - dom * CELLS
        tile = (local >> 14) * TILES + ((local >> 7) & (TILES - 1))
        return (tile * LEVELS + ((local >> 11) & (LEVELS - 1))) * LANES + (local & (LANES - 1))

    def rows_of(x, t):
        return pl.ds(pl.multiple_of(((x - 1) * TILES + t) * LEVELS, LEVELS), LEVELS)

    def first_step(s, x, sides, new_wave, new_adj):
        at = source_of(s) - (x - 1) * (TILES * LEVELS * LANES)
        wavelet = source_wave[0, s]
        pair = zip(laplace(wave0, s, x, sides), laplace(adj0, s, x, sides), strict=True)
        for t, ((wave, wave_lap), (adj, adj_lap)) in enumerate(pair):
            cols = columns_of(t)
            v = vel[x - 1, :, cols]
            pushed = v * wave_lap + jnp.where(place == at - t * (LEVELS * LANES), wavelet, 0.0)
            new_wave[:, cols] = (2.0 * wave - prev[s, x - 1, :, cols]) + pushed
            prev[s, x - 1, :, cols] = pushed
            drawn = injected[s, rows_of(x, t), pl.ds(0, LANES)]
            new_adj[:, cols] = (2.0 * adj - after[s, x - 1, :, cols]) + (v * adj_lap + drawn)

    def second_step(s, x, total, place_x):
        at = source_of(s) - (x - 1) * (TILES * LEVELS * LANES)
        wavelet = source_wave[1, s]
        inside = aperture[s, 0] == dom
        for k in range(1, 8):
            inside = inside | (aperture[s, k] == dom)
        weight = jnp.where(inside, scale, 0.0)
        pair = zip(laplace(wave1, s, x), laplace(adj1, s, x), strict=True)
        for t, ((_, wave_lap), (adj, adj_lap)) in enumerate(pair):
            cols = columns_of(t)
            v = vel[x - 1, :, cols]
            pushed = v * wave_lap + jnp.where(place == at - t * (LEVELS * LANES), wavelet, 0.0)
            drawn = injected[s, rows_of(x, t), pl.ds(LANES, LANES)]
            zero = (2.0 * adj - adj0[s, x, :, cols]) + (v * adj_lap + drawn)
            image = weight * (adj * pushed + zero * prev[s, x - 1, :, cols])
            total[place_x, :, cols] += image

    def inject(s):
        local = cells_ref[pl.ds(s, 1), :] - dom * CELLS
        tile = (local >> 14) * TILES + ((local >> 7) & (TILES - 1))
        line = tile * LEVELS + ((local >> 11) & (LEVELS - 1))
        spot = local & (LANES - 1)
        lines = PLANES * TILES * LEVELS
        picks = lax.broadcasted_iota(jnp.int32, (lines, RECEIVERS), 0) == line
        picks = jnp.where(picks, 1.0, 0.0).astype(jnp.bfloat16)
        hits = lax.broadcasted_iota(jnp.int32, (LANES, RECEIVERS), 0) == spot
        parts = []
        for step in (0, 1):
            rest = residual_ref[s, pl.ds(step, 1), :]
            pieces = []
            for _ in range(3):
                piece = rest.astype(jnp.bfloat16).astype(jnp.float32)
                rest = rest - piece
                pieces.append(jnp.where(hits, piece, 0.0).astype(jnp.bfloat16))
            parts.append(jnp.concatenate(pieces, axis=1))
        injected[s] = lax.dot_general(
            jnp.concatenate([picks] * 3, axis=1),
            jnp.concatenate(parts, axis=0),
            (((1,), (1,)), ((), ())),
            preferred_element_type=jnp.float32,
        )

    def planes(first, last, body):
        def step(x, carry):
            body(x)
            return carry

        lax.fori_loop(first, last, step, 0)

    def end_plane(way):
        return 1 + (1 - way) * (PLANES - 1)

    def ghost_plane(way):
        return (1 - way) * (PLANES + 1)

    for copy in small_loads:
        copy.wait()

    def phase_one(s):
        advance(0, s)
        inject(s)
        for copy in load(s):
            copy.wait()

        def part(way):
            x = end_plane(way)
            first_step(s, x, (2 + (1 - way) * (PLANES - 3),), ends.at[way, 0, s], ends.at[way, 1, s])

        planes(0, 2, part)
        send_first_legs(2, s)
        send_first_legs(3, s)

    each_shot(phase_one)

    def phase_two(s):
        advance(1, s)

        def plane(x):
            first_step(s, x, (x - 1, x + 1), wave1.at[s, x], adj1.at[s, x])

        planes(2, PLANES, plane)

    each_shot(phase_two)

    def clear_inner(x):
        inner[x] = jnp.zeros((LEVELS, COLUMNS), jnp.float32)

    planes(0, PLANES - 2, clear_inner)

    def phase_three(s):
        advance(2, s)
        take_layer(0, s)
        take_layer(1, s)

        def complete(way):
            x, ghost = end_plane(way), ghost_plane(way)
            v = vel[x - 1]
            pushed = v * wave0[s, ghost]
            wave1[s, x] = ends[way, 0, s] + pushed
            prev[s, x - 1] += pushed
            adj1[s, x] = ends[way, 1, s] + v * adj0[s, ghost]

        planes(0, 2, complete)
        planes(2, PLANES, lambda x: second_step(s, x, inner, x - 2))

    each_shot(phase_three)

    def eighth_of(index):
        return pl.ds(pl.multiple_of(index * EIGHTH, EIGHTH), EIGHTH)

    def scatter(k):
        peer = lax.rem(eighth + k, 8)
        return remote(
            inner.at[:, :, eighth_of(peer)],
            inner_got.at[k],
            red_send.at[k],
            red_recv.at[k],
            member(peer),
        )

    def gather(k):
        mine = out_ref.at[pl.ds(1, PLANES - 2), :, eighth_of(eighth)]
        return remote(
            mine, mine, gather_send.at[k], gather_recv.at[k], member(lax.rem(eighth + k, 8))
        )

    def gathered(k):
        peer = lax.rem(eighth - k + 8, 8)
        there = out_ref.at[pl.ds(1, PLANES - 2), :, eighth_of(peer)]
        return remote(there, there, gather_send.at[k], gather_recv.at[k], member(peer))

    def every(count, body):
        def step(k, carry):
            body(k)
            return carry

        lax.fori_loop(1, count, step, 0)

    every(8, lambda k: scatter(k).start())

    def clear_edge(x):
        edge[x] = jnp.zeros((LEVELS, COLUMNS), jnp.float32)

    planes(0, 2, clear_edge)

    def ends_second(s):
        take_layer(2, s)
        take_layer(3, s)

        def part(way):
            x, ghost = end_plane(way), ghost_plane(way)
            v = vel_ghost[1 - way]
            wave1[s, ghost] += v * wave0[s, x]
            adj1[s, ghost] += v * adj0[s, x]
            second_step(s, x, edge, 1 - way)

        planes(0, 2, part)

    def swap():
        return remote(
            inner_part,
            pair_got,
            pair_sem.at[0],
            pair_sem.at[1],
            {"shot": shot + 2 - 4 * lower},
        )

    def add_inner(k):
        scatter(k).wait_recv()
        inner_part[...] += inner_got[k]

    def sum_inner():
        inner_part[...] = inner[:, :, eighth_of(eighth)]
        every(8, add_inner)
        swap().start()

    def share_inner():
        swap().wait_recv()
        out_ref[pl.ds(1, PLANES - 2), :, eighth_of(eighth)] = inner_part[...] + pair_got[...]
        every(8, lambda k: gather(k).start())

    when_each(from_has, lambda way: vel_layer(way).wait_recv())

    def phase_four(s, carry):
        pl.when(s < SHOTS)(lambda: advance(3, s))
        pl.when(s == 2)(sum_inner)
        pl.when(s == 4)(share_inner)
        pl.when(s >= 2)(lambda: ends_second(s - 2))
        return carry

    lax.fori_loop(0, SHOTS + 2, phase_four, 0)

    def lane_tile(index):
        return pl.ds(pl.multiple_of(index * LANES, LANES), LANES)

    def scatter_edge(k):
        peer = lax.rem(shot + k, GROUP)
        return remote(
            edge.at[:, :, lane_tile(peer)],
            edge_got.at[k],
            edge_send.at[k],
            edge_recv.at[k],
            {"shot": peer},
        )

    def spread(k):
        mine = edge_out.at[:, :, lane_tile(shot)]
        return remote(
            mine, mine, spread_send.at[k], spread_recv.at[k], {"shot": lax.rem(shot + k, GROUP)}
        )

    def spread_from(k):
        peer = lax.rem(shot - k + GROUP, GROUP)
        there = edge_out.at[:, :, lane_tile(peer)]
        return remote(there, there, spread_send.at[k], spread_recv.at[k], {"shot": peer})

    every(GROUP, lambda k: scatter_edge(k).start())

    def add_edge(k, carry):
        scatter_edge(k).wait_recv()
        return carry + edge_got[k]

    edge_out[:, :, lane_tile(shot)] = lax.fori_loop(1, GROUP, add_edge, edge[:, :, lane_tile(shot)])
    every(GROUP, lambda k: spread(k).start())

    for k in range(4):
        each_shot(functools.partial(end_legs, k))
    when_each(has, lambda way: vel_layer(way).wait_send())
    swap().wait_send()
    every(8, lambda k: scatter(k).wait_send())
    every(8, lambda k: gather(k).wait_send())
    every(8, lambda k: gathered(k).wait_recv())
    every(GROUP, lambda k: scatter_edge(k).wait_send())
    every(GROUP, lambda k: spread(k).wait_send())
    every(GROUP, lambda k: spread_from(k).wait_recv())
    out_ref[0] = edge_out[0]
    out_ref[PLANES - 1] = edge_out[1]


def body(*arguments):
    arguments = (*arguments[:6], arguments[6].T, *arguments[7:])
    scale = float(lax.axis_size("shot") * SHOTS) ** (-0.5)
    f32 = jnp.float32
    block = (LEVELS, COLUMNS)
    dma = pltpu.SemaphoreType.DMA
    hbm = pl.BlockSpec(memory_space=pltpu.HBM)
    return pl.pallas_call(
        functools.partial(kernel, scale),
        out_shape=jax.ShapeDtypeStruct((PLANES, *block), f32),
        in_specs=[hbm] * 10,
        out_specs=pl.BlockSpec(memory_space=pltpu.VMEM),
        scratch_shapes=[
            pltpu.SMEM((SHOTS,), jnp.int32),
            pltpu.SMEM((2, SHOTS), f32),
            pltpu.VMEM((SHOTS, RECEIVERS), jnp.int32),
            pltpu.VMEM((SHOTS, 2, RECEIVERS), f32),
            pltpu.SMEM((SHOTS, 8), jnp.int32),
            pltpu.VMEM((PLANES, *block), f32),
            pltpu.VMEM((SHOTS, PLANES + 2, *block), f32),
            pltpu.VMEM((SHOTS, PLANES + 2, *block), f32),
            pltpu.VMEM((SHOTS, PLANES + 2, *block), f32),
            pltpu.VMEM((SHOTS, PLANES + 2, *block), f32),
            pltpu.VMEM((SHOTS, PLANES, *block), f32),
            pltpu.VMEM((SHOTS, PLANES, *block), f32),
            pltpu.VMEM((SHOTS, CELLS // LANES, 2 * LANES), f32),
            pltpu.VMEM((PLANES - 2, *block), f32),
            pltpu.VMEM((2, *block), f32),
            pltpu.VMEM((2, *block), f32),
            pltpu.VMEM((2, 2, SHOTS, *block), f32),
            pltpu.VMEM((2, *block), f32),
            pltpu.VMEM((4, SHOTS, LEVELS, HALF), f32),
            pltpu.VMEM((8, PLANES - 2, LEVELS, EIGHTH), f32),
            pltpu.VMEM((PLANES - 2, LEVELS, EIGHTH), f32),
            pltpu.VMEM((PLANES - 2, LEVELS, EIGHTH), f32),
            pltpu.VMEM((GROUP, 2, LEVELS, LANES), f32),
            dma((SHOTS, 4)),
            dma((6,)),
            dma((2,)),
            dma((2,)),
            dma((2, 4, SHOTS)),
            dma((2, 4, SHOTS)),
            dma((2, 4, SHOTS)),
            dma((2, 4, SHOTS)),
            dma((8,)),
            dma((8,)),
            dma((2,)),
            dma((8,)),
            dma((8,)),
            dma((GROUP,)),
            dma((GROUP,)),
            dma((GROUP,)),
            dma((GROUP,)),
        ],
        compiler_params=pltpu.CompilerParams(
            collective_id=0, has_side_effects=True, vmem_limit_bytes=64 * 2**20
        ),
        name="gradient",
    )(*arguments)


def solution(mesh):
    placed = (
        P("dom", None, None),
        P("shot", "dom", None, None),
        P("shot", "dom", None, None),
        P("shot", "dom", None, None),
        P("shot", "dom", None, None),
        P("shot"),
        P("shot", None),
        P("shot", None),
        P("shot", None, None),
        P("shot", None),
    )
    return jax.shard_map(
        body, mesh=mesh, in_specs=placed, out_specs=P("dom", None, None), check_vma=False
    )
```

```python
import functools

import jax
import jax.numpy as jnp
from jax import lax
from jax.experimental import pallas as pl
from jax.experimental.pallas import tpu as pltpu
from jax.sharding import PartitionSpec as P

MESH = pl.DeviceIdType.MESH
SHOTS = 4
PLANES = 8
LEVELS = 8
COLUMNS = 2048
LANES = 128
TILES = COLUMNS // LANES
RECEIVERS = 256
GROUP = 16
HALF = COLUMNS // 2
CELLS = PLANES * LEVELS * COLUMNS
EIGHTH = COLUMNS // 8
MIDDLE = PLANES - 4
WINDOW = 2
UP, DOWN = 0, 1
ENDS = (PLANES, 1)
GHOSTS = (0, PLANES + 1)


def kernel(
    scale,
    vel_hbm,
    wave_prev_hbm,
    wave_now_hbm,
    adj_next_hbm,
    adj_now_hbm,
    source_cell_hbm,
    source_wave_hbm,
    cells_hbm,
    residual_hbm,
    aperture_hbm,
    out_ref,
    source_cell,
    source_wave,
    cells_ref,
    residual_ref,
    aperture,
    vel,
    wave0,
    wave1,
    adj0,
    adj1,
    prev,
    after,
    injected,
    inner,
    beside,
    beside_out,
    outer,
    outer_got,
    outer_out,
    ends,
    vel_ghost,
    relay_buf,
    inner_got,
    inner_part,
    inner_pair,
    beside_got,
    beside_part,
    beside_pair,
    load_sem,
    small_sem,
    vel_send,
    vel_recv,
    share_send,
    share_recv,
    send_sem,
    recv_sem,
    relay_send,
    relay_recv,
    red_send,
    red_recv,
    pair_sem,
    gather_send,
    gather_recv,
    outer_send,
    outer_recv,
    spread_send,
    spread_recv,
):
    shot = lax.axis_index("shot")
    dom = lax.axis_index("dom")
    column = lax.rem(dom, 4)
    row = dom // 4
    lower = lax.rem(shot // 2, 2)
    eighth = (shot // 4) * 2 + lax.rem(shot, 2)

    def along_dom(step):
        return {"dom": lax.rem(dom + step + GROUP, GROUP)}

    def member(index):
        return {"shot": (index // 2) * 4 + lower * 2 + lax.rem(index, 2)}

    towards = (along_dom(1), along_dom(-1))
    has = (dom < GROUP - 1, dom > 0)
    from_has = (dom > 0, dom < GROUP - 1)
    crosses = (column == 3, column == 0)
    from_crosses = (column == 0, column == 3)
    relays = ((column == 0) & (row < 3), (column == 3) & (row > 0))
    relay_first = (along_dom(-3), along_dom(3))
    relay_second = (along_dom(4), along_dom(-4))

    def load(s):
        return [
            pltpu.make_async_copy(source.at[s], target, load_sem.at[s, k])
            for k, (source, target) in enumerate(
                (
                    (wave_now_hbm, wave0.at[s, pl.ds(1, PLANES)]),
                    (adj_now_hbm, adj0.at[s, pl.ds(1, PLANES)]),
                    (wave_prev_hbm, prev.at[s]),
                    (adj_next_hbm, after.at[s]),
                )
            )
        ]

    small_loads = [
        pltpu.make_async_copy(source, target, small_sem.at[k])
        for k, (source, target) in enumerate(
            (
                (cells_hbm, cells_ref),
                (residual_hbm, residual_ref),
                (vel_hbm, vel),
                (source_cell_hbm, source_cell),
                (source_wave_hbm, source_wave),
                (aperture_hbm, aperture),
            )
        )
    ]
    for copy in small_loads:
        copy.start()
    for s in range(SHOTS):
        for copy in load(s):
            copy.start()

    barrier = pltpu.get_barrier_semaphore()

    def greet(device):
        pl.semaphore_signal(barrier, inc=1, device_id=device, device_id_type=MESH)

    def greet_peer(k, carry):
        greet({"shot": lax.rem(shot + k, GROUP)})
        return carry

    lax.fori_loop(1, GROUP, greet_peer, 0)
    greet(towards[UP])
    greet(towards[DOWN])

    @pl.when(column == 0)
    def _():
        greet(along_dom(3))
        greet(along_dom(4))
        greet(along_dom(-4))

    @pl.when(column == 3)
    def _():
        greet(along_dom(-3))
        greet(along_dom(4))
        greet(along_dom(-4))

    relaying = (column == 0) | (column == 3)
    pl.semaphore_wait(barrier, GROUP + 1 + jnp.where(relaying, 3, 0))

    fields = ((wave_now_hbm, wave0), (adj_now_hbm, adj0), (None, wave1), (None, adj1))

    def layer_refs(k, s, way):
        given, block = fields[k]
        source = ends.at[way, k - 2, s] if given is None else given.at[s, ENDS[way] - 1]
        return source, block.at[s, GHOSTS[way]]

    def remote(source, target, send, recv, device):
        return pltpu.make_async_remote_copy(
            src_ref=source,
            dst_ref=target,
            send_sem=send,
            recv_sem=recv,
            device_id=device,
            device_id_type=MESH,
        )

    first_half, second_half = pl.ds(0, HALF), pl.ds(HALF, HALF)

    def whole(k, s, way):
        source, target = layer_refs(k, s, way)
        return remote(source, target, send_sem.at[way, k, s], recv_sem.at[way, k, s], towards[way])

    def direct(k, s, way):
        source, target = layer_refs(k, s, way)
        return remote(
            source.at[:, first_half],
            target.at[:, first_half],
            send_sem.at[way, k, s],
            recv_sem.at[way, k, s],
            towards[way],
        )

    def leg_one(k, s, way):
        source, _ = layer_refs(k, s, way)
        return remote(
            source.at[:, second_half],
            relay_buf.at[k, s],
            relay_send.at[0, k, s],
            relay_recv.at[0, k, s],
            relay_first[way],
        )

    def leg_two(k, s, way):
        _, target = layer_refs(k, s, way)
        return remote(
            relay_buf.at[k, s],
            target.at[:, second_half],
            relay_send.at[1, k, s],
            relay_recv.at[1, k, s],
            relay_second[way],
        )

    def when_each(conditions, body):
        for way in (UP, DOWN):
            pl.when(conditions[way])(functools.partial(body, way))

    def both(one, other):
        return tuple(a & b for a, b in zip(one, other, strict=True))

    def but(one, other):
        return tuple(a & jnp.logical_not(b) for a, b in zip(one, other, strict=True))

    far, near = both(has, crosses), but(has, crosses)
    from_far, from_near = both(from_has, from_crosses), but(from_has, from_crosses)

    def send_first_legs(k, s):
        when_each(far, lambda way: leg_one(k, s, way).start())

    def send_layer(k, s):
        when_each(far, lambda way: direct(k, s, way).start())
        when_each(near, lambda way: whole(k, s, way).start())

    def advance(k, s):
        when_each(far, lambda way: direct(k, s, way).wait_send())
        when_each(near, lambda way: whole(k, s, way).wait_send())
        pl.when(s < SHOTS - WINDOW)(lambda: send_layer(k, s + WINDOW))
        if k < 3:
            pl.when(s >= SHOTS - WINDOW)(lambda: send_layer(k + 1, s + WINDOW - SHOTS))

        def pass_on(way):
            leg_one(k, s, way).wait_recv()
            leg_two(k, s, way).start()

        when_each(relays, pass_on)

    def take_layer(k, s):
        def two_halves(way):
            direct(k, s, way).wait_recv()
            leg_two(k, s, way).wait_recv()

        when_each(from_far, two_halves)
        when_each(from_near, lambda way: whole(k, s, way).wait_recv())

    def end_legs(k, s):
        when_each(far, lambda way: leg_one(k, s, way).wait_send())
        when_each(relays, lambda way: leg_two(k, s, way).wait_send())

    def eighth_of(index):
        return pl.ds(pl.multiple_of(index * EIGHTH, EIGHTH), EIGHTH)

    def vel_piece(way):
        return remote(
            vel_hbm.at[ENDS[way] - 1, :, eighth_of(eighth)],
            vel_ghost.at[way, :, eighth_of(eighth)],
            vel_send.at[way],
            vel_recv.at[way],
            towards[way],
        )

    def share_vel(k):
        mine = vel_ghost.at[:, :, eighth_of(eighth)]
        peer = member(lax.rem(eighth + k, 8))
        return remote(mine, mine, share_send.at[k], share_recv.at[k], peer)

    def shared_vel(k):
        peer = lax.rem(eighth - k + 8, 8)
        there = vel_ghost.at[:, :, eighth_of(peer)]
        return remote(there, there, share_send.at[k], share_recv.at[k], member(peer))

    eighths = range(1, 8)

    def each_shot(body):
        def step(s, carry):
            body(s)
            return carry

        lax.fori_loop(0, SHOTS, step, 0)

    for k in (0, 1):
        each_shot(functools.partial(send_first_legs, k))
    when_each(has, lambda way: vel_piece(way).start())
    for s in range(WINDOW):
        send_layer(0, s)

    def clear_ghosts(way):
        nothing = jnp.zeros((LEVELS, COLUMNS), jnp.float32)
        vel_ghost[way, :, eighth_of(eighth)] = jnp.zeros((LEVELS, EIGHTH), jnp.float32)

        def clear(s):
            for block in (wave0, adj0, wave1, adj1):
                block[s, GHOSTS[way]] = nothing

        each_shot(clear)

    when_each(tuple(jnp.logical_not(there) for there in from_has), clear_ghosts)

    level = lax.broadcasted_iota(jnp.int32, (LEVELS, LANES), 0)
    lane = lax.broadcasted_iota(jnp.int32, (LEVELS, LANES), 1)
    place = level * LANES + lane
    top, bottom = level == 0, level == LEVELS - 1
    leftmost, rightmost = lane == 0, lane == LANES - 1

    def columns_of(t):
        return pl.ds(t * LANES, LANES)

    def laplace(ref, s, x, sides=None):
        sides = (x - 1, x + 1) if sides is None else sides
        empty = jnp.zeros((LEVELS, LANES), jnp.float32)
        here = ref[s, x, :, columns_of(0)]
        right_of = pltpu.roll(here, LANES - 1, 1)
        before = empty
        for t in range(TILES):
            if t + 1 < TILES:
                following = ref[s, x, :, columns_of(t + 1)]
                right_next = pltpu.roll(following, LANES - 1, 1)
            else:
                following, right_next = empty, empty
            shifted = pltpu.roll(here, 1, 1)
            left = jnp.where(leftmost, before, shifted)
            right = jnp.where(rightmost, right_next, right_of)
            above = jnp.where(top, 0.0, pltpu.roll(here, 1, 0))
            below = jnp.where(bottom, 0.0, pltpu.roll(here, LEVELS - 1, 0))
            beside = (above + below) + (left + right)
            for side in sides:
                beside = beside + ref[s, side, :, columns_of(t)]
            yield here, beside - 6.0 * here
            before, here, right_of = shifted, following, right_next

    def source_of(s):
        local = source_cell[s] - dom * CELLS
        tile = (local >> 14) * TILES + ((local >> 7) & (TILES - 1))
        return (tile * LEVELS + ((local >> 11) & (LEVELS - 1))) * LANES + (local & (LANES - 1))

    def rows_of(x, t):
        return pl.ds(pl.multiple_of(((x - 1) * TILES + t) * LEVELS, LEVELS), LEVELS)

    def first_step(s, x, sides, new_wave, new_adj):
        at = source_of(s) - (x - 1) * (TILES * LEVELS * LANES)
        wavelet = source_wave[0, s]
        pair = zip(laplace(wave0, s, x, sides), laplace(adj0, s, x, sides), strict=True)
        for t, ((wave, wave_lap), (adj, adj_lap)) in enumerate(pair):
            cols = columns_of(t)
            v = vel[x - 1, :, cols]
            pushed = v * wave_lap + jnp.where(place == at - t * (LEVELS * LANES), wavelet, 0.0)
            new_wave[:, cols] = (2.0 * wave - prev[s, x - 1, :, cols]) + pushed
            prev[s, x - 1, :, cols] = pushed
            drawn = injected[s, rows_of(x, t), pl.ds(0, LANES)]
            new_adj[:, cols] = (2.0 * adj - after[s, x - 1, :, cols]) + (v * adj_lap + drawn)

    def second_step(s, x, add):
        at = source_of(s) - (x - 1) * (TILES * LEVELS * LANES)
        wavelet = source_wave[1, s]
        inside = aperture[s, 0] == dom
        for k in range(1, 8):
            inside = inside | (aperture[s, k] == dom)
        weight = jnp.where(inside, scale, 0.0)
        pair = zip(laplace(wave1, s, x), laplace(adj1, s, x), strict=True)
        for t, ((_, wave_lap), (adj, adj_lap)) in enumerate(pair):
            cols = columns_of(t)
            v = vel[x - 1, :, cols]
            pushed = v * wave_lap + jnp.where(place == at - t * (LEVELS * LANES), wavelet, 0.0)
            drawn = injected[s, rows_of(x, t), pl.ds(LANES, LANES)]
            zero = (2.0 * adj - adj0[s, x, :, cols]) + (v * adj_lap + drawn)
            image = weight * (adj * pushed + zero * prev[s, x - 1, :, cols])
            add(t, image)

    def inject(s):
        local = cells_ref[pl.ds(s, 1), :] - dom * CELLS
        tile = (local >> 14) * TILES + ((local >> 7) & (TILES - 1))
        line = tile * LEVELS + ((local >> 11) & (LEVELS - 1))
        spot = local & (LANES - 1)
        lines = PLANES * TILES * LEVELS
        picks = lax.broadcasted_iota(jnp.int32, (lines, RECEIVERS), 0) == line
        picks = jnp.where(picks, 1.0, 0.0).astype(jnp.bfloat16)
        hits = lax.broadcasted_iota(jnp.int32, (LANES, RECEIVERS), 0) == spot
        parts = []
        for step in (0, 1):
            rest = residual_ref[s, pl.ds(step, 1), :]
            pieces = []
            for _ in range(3):
                piece = rest.astype(jnp.bfloat16).astype(jnp.float32)
                rest = rest - piece
                pieces.append(jnp.where(hits, piece, 0.0).astype(jnp.bfloat16))
            parts.append(jnp.concatenate(pieces, axis=1))
        injected[s] = lax.dot_general(
            jnp.concatenate([picks] * 3, axis=1),
            jnp.concatenate(parts, axis=0),
            (((1,), (1,)), ((), ())),
            preferred_element_type=jnp.float32,
        )

    def planes(first, last, body):
        def step(x, carry):
            body(x)
            return carry

        lax.fori_loop(first, last, step, 0)

    def end_plane(way):
        return 1 + (1 - way) * (PLANES - 1)

    def ghost_plane(way):
        return (1 - way) * (PLANES + 1)

    for copy in small_loads:
        copy.wait()

    def phase_one(s):
        advance(0, s)
        inject(s)
        for copy in load(s):
            copy.wait()

        def part(way):
            x = end_plane(way)
            first_step(s, x, (2 + (1 - way) * (PLANES - 3),), ends.at[way, 0, s], ends.at[way, 1, s])

        planes(0, 2, part)
        send_first_legs(2, s)
        send_first_legs(3, s)

    each_shot(phase_one)

    def clear_inner(x):
        inner[x] = jnp.zeros((LEVELS, COLUMNS), jnp.float32)

    def clear_outer(t):
        outer[t] = jnp.zeros((2, LEVELS, LANES), jnp.float32)

    def clear_beside(way):
        beside[way] = jnp.zeros((LEVELS, COLUMNS), jnp.float32)

    planes(0, MIDDLE, clear_inner)
    planes(0, 2, clear_beside)
    planes(0, TILES, clear_outer)
    when_each(from_has, lambda way: vel_piece(way).wait_recv())
    for k in eighths:
        share_vel(k).start()

    def phase_two(s):
        advance(1, s)

        def plane(x):
            first_step(s, x, (x - 1, x + 1), wave1.at[s, x], adj1.at[s, x])

        planes(2, PLANES, plane)

        def middle(x):
            def add(t, image):
                inner[x - 3, :, columns_of(t)] += image

            second_step(s, x, add)

        planes(3, PLANES - 1, middle)

    each_shot(phase_two)

    sets = (
        (inner, inner_got, inner_part, inner_pair, out_ref.at[pl.ds(2, MIDDLE)]),
        (beside, beside_got, beside_part, beside_pair, beside_out),
    )

    def scatter(which, k):
        total, got, _, _, _ = sets[which]
        peer = lax.rem(eighth + k, 8)
        return remote(
            total.at[:, :, eighth_of(peer)],
            got.at[k],
            red_send.at[which, k],
            red_recv.at[which, k],
            member(peer),
        )

    def swap(which):
        _, _, part, pair, _ = sets[which]
        return remote(
            part,
            pair,
            pair_sem.at[which, 0],
            pair_sem.at[which, 1],
            {"shot": shot + 2 - 4 * lower},
        )

    def gather(which, k):
        mine = sets[which][4].at[:, :, eighth_of(eighth)]
        return remote(
            mine,
            mine,
            gather_send.at[which, k],
            gather_recv.at[which, k],
            member(lax.rem(eighth + k, 8)),
        )

    def gathered(which, k):
        peer = lax.rem(eighth - k + 8, 8)
        there = sets[which][4].at[:, :, eighth_of(peer)]
        return remote(
            there, there, gather_send.at[which, k], gather_recv.at[which, k], member(peer)
        )

    def start_sum(which):
        for k in eighths:
            scatter(which, k).start()

    def add_up(which):
        total, got, part, _, _ = sets[which]
        value = total[:, :, eighth_of(eighth)]
        for k in eighths:
            scatter(which, k).wait_recv()
            value = value + got[k]
        part[...] = value
        swap(which).start()

    def give_back(which):
        _, _, part, pair, result = sets[which]
        swap(which).wait_recv()
        result[:, :, eighth_of(eighth)] = part[...] + pair[...]
        for k in eighths:
            gather(which, k).start()

    def end_sum(which):
        swap(which).wait_send()
        for k in eighths:
            scatter(which, k).wait_send()
            gather(which, k).wait_send()
            gathered(which, k).wait_recv()

    def scatter_outer(k):
        peer = lax.rem(shot + k, GROUP)
        return remote(
            outer.at[peer], outer_got.at[k], outer_send.at[k], outer_recv.at[k], {"shot": peer}
        )

    def spread(k):
        mine = outer_out.at[shot]
        return remote(
            mine, mine, spread_send.at[k], spread_recv.at[k], {"shot": lax.rem(shot + k, GROUP)}
        )

    def spread_from(k):
        peer = lax.rem(shot - k + GROUP, GROUP)
        there = outer_out.at[peer]
        return remote(there, there, spread_send.at[k], spread_recv.at[k], {"shot": peer})

    peers = range(1, GROUP)

    def start_outer():
        for k in peers:
            scatter_outer(k).start()

    def sum_outer():
        total = outer[shot]
        for k in peers:
            scatter_outer(k).wait_recv()
            total = total + outer_got[k]
        outer_out[shot] = total
        for k in peers:
            spread(k).start()

    def end_outer():
        for k in peers:
            scatter_outer(k).wait_send()
            spread(k).wait_send()
        for k in peers:
            spread_from(k).wait_recv()
        for t in range(TILES):
            for side in (0, 1):
                out_ref[side * (PLANES - 1), :, columns_of(t)] = outer_out[t, side]

    start_sum(0)

    def phase_three(s):
        advance(2, s)
        take_layer(0, s)
        take_layer(1, s)

        def complete(way):
            x, ghost = end_plane(way), ghost_plane(way)
            v = vel[x - 1]
            pushed = v * wave0[s, ghost]
            wave1[s, x] = ends[way, 0, s] + pushed
            prev[s, x - 1] += pushed
            adj1[s, x] = ends[way, 1, s] + v * adj0[s, ghost]

        planes(0, 2, complete)

        def next_to(way):
            def add(t, image):
                beside[1 - way, :, columns_of(t)] += image

            second_step(s, 2 + (1 - way) * (PLANES - 3), add)

        planes(0, 2, next_to)

    each_shot(phase_three)
    start_sum(1)

    def ends_second(s):
        take_layer(2, s)
        take_layer(3, s)

        def part(way):
            x, ghost = end_plane(way), ghost_plane(way)
            v = vel_ghost[1 - way]
            wave1[s, ghost] += v * wave0[s, x]
            adj1[s, ghost] += v * adj0[s, x]

            def add(t, image):
                outer[t, 1 - way] += image

            second_step(s, x, add)

        planes(0, 2, part)

    advance(3, 0)
    advance(3, 1)
    add_up(0)
    advance(3, 2)
    advance(3, 3)
    give_back(0)
    for k in eighths:
        shared_vel(k).wait_recv()
    add_up(1)

    each_shot(ends_second)
    start_outer()
    give_back(1)
    end_sum(0)
    sum_outer()
    end_sum(1)
    out_ref[1] = beside_out[0]
    out_ref[PLANES - 2] = beside_out[1]

    for k in range(4):
        each_shot(functools.partial(end_legs, k))
    when_each(has, lambda way: vel_piece(way).wait_send())
    for k in eighths:
        share_vel(k).wait_send()
    end_outer()


def body(*arguments):
    arguments = (*arguments[:6], arguments[6].T, *arguments[7:])
    scale = float(lax.axis_size("shot") * SHOTS) ** (-0.5)
    f32 = jnp.float32
    block = (LEVELS, COLUMNS)
    dma = pltpu.SemaphoreType.DMA
    hbm = pl.BlockSpec(memory_space=pltpu.HBM)
    return pl.pallas_call(
        functools.partial(kernel, scale),
        out_shape=jax.ShapeDtypeStruct((PLANES, *block), f32),
        in_specs=[hbm] * 10,
        out_specs=pl.BlockSpec(memory_space=pltpu.VMEM),
        scratch_shapes=[
            pltpu.SMEM((SHOTS,), jnp.int32),
            pltpu.SMEM((2, SHOTS), f32),
            pltpu.VMEM((SHOTS, RECEIVERS), jnp.int32),
            pltpu.VMEM((SHOTS, 2, RECEIVERS), f32),
            pltpu.SMEM((SHOTS, 8), jnp.int32),
            pltpu.VMEM((PLANES, *block), f32),
            pltpu.VMEM((SHOTS, PLANES + 2, *block), f32),
            pltpu.VMEM((SHOTS, PLANES + 2, *block), f32),
            pltpu.VMEM((SHOTS, PLANES + 2, *block), f32),
            pltpu.VMEM((SHOTS, PLANES + 2, *block), f32),
            pltpu.VMEM((SHOTS, PLANES, *block), f32),
            pltpu.VMEM((SHOTS, PLANES, *block), f32),
            pltpu.VMEM((SHOTS, CELLS // LANES, 2 * LANES), f32),
            pltpu.VMEM((MIDDLE, *block), f32),
            pltpu.VMEM((2, *block), f32),
            pltpu.VMEM((2, *block), f32),
            pltpu.VMEM((TILES, 2, LEVELS, LANES), f32),
            pltpu.VMEM((TILES, 2, LEVELS, LANES), f32),
            pltpu.VMEM((TILES, 2, LEVELS, LANES), f32),
            pltpu.VMEM((2, 2, SHOTS, *block), f32),
            pltpu.VMEM((2, *block), f32),
            pltpu.VMEM((4, SHOTS, LEVELS, HALF), f32),
            pltpu.VMEM((8, MIDDLE, LEVELS, EIGHTH), f32),
            pltpu.VMEM((MIDDLE, LEVELS, EIGHTH), f32),
            pltpu.VMEM((MIDDLE, LEVELS, EIGHTH), f32),
            pltpu.VMEM((8, 2, LEVELS, EIGHTH), f32),
            pltpu.VMEM((2, LEVELS, EIGHTH), f32),
            pltpu.VMEM((2, LEVELS, EIGHTH), f32),
            dma((SHOTS, 4)),
            dma((6,)),
            dma((2,)),
            dma((2,)),
            dma((8,)),
            dma((8,)),
            dma((2, 4, SHOTS)),
            dma((2, 4, SHOTS)),
            dma((2, 4, SHOTS)),
            dma((2, 4, SHOTS)),
            dma((2, 8)),
            dma((2, 8)),
            dma((2, 2)),
            dma((2, 8)),
            dma((2, 8)),
            dma((GROUP,)),
            dma((GROUP,)),
            dma((GROUP,)),
            dma((GROUP,)),
        ],
        compiler_params=pltpu.CompilerParams(
            collective_id=0, has_side_effects=True, vmem_limit_bytes=64 * 2**20
        ),
        name="gradient",
    )(*arguments)


def solution(mesh):
    placed = (
        P("dom", None, None),
        P("shot", "dom", None, None),
        P("shot", "dom", None, None),
        P("shot", "dom", None, None),
        P("shot", "dom", None, None),
        P("shot"),
        P("shot", None),
        P("shot", None),
        P("shot", None, None),
        P("shot", None),
    )
    return jax.shard_map(
        body, mesh=mesh, in_specs=placed, out_specs=P("dom", None, None), check_vma=False
    )
```

```python
import functools

import jax
import jax.numpy as jnp
from jax import lax
from jax.experimental import pallas as pl
from jax.experimental.pallas import tpu as pltpu
from jax.sharding import PartitionSpec as P

MESH = pl.DeviceIdType.MESH
SHOTS = 4
PLANES = 8
LEVELS = 8
COLUMNS = 2048
LANES = 128
TILES = COLUMNS // LANES
RECEIVERS = 256
GROUP = 16
HALF = COLUMNS // 2
CELLS = PLANES * LEVELS * COLUMNS
EIGHTH = COLUMNS // 8
MIDDLE = PLANES - 4
WINDOW = 2
UP, DOWN = 0, 1
ENDS = (PLANES, 1)
GHOSTS = (0, PLANES + 1)


def kernel(
    scale,
    vel_hbm,
    wave_prev_hbm,
    wave_now_hbm,
    adj_next_hbm,
    adj_now_hbm,
    source_cell_hbm,
    source_wave_hbm,
    cells_hbm,
    residual_hbm,
    aperture_hbm,
    out_ref,
    source_cell,
    source_wave,
    cells_ref,
    residual_ref,
    aperture,
    vel,
    wave0,
    wave1,
    adj0,
    adj1,
    prev,
    after,
    injected,
    inner,
    beside,
    beside_out,
    outer,
    outer_got,
    outer_out,
    ends,
    vel_ghost,
    relay_buf,
    inner_got,
    inner_part,
    inner_pair,
    beside_got,
    beside_part,
    beside_pair,
    load_sem,
    small_sem,
    vel_send,
    vel_recv,
    share_send,
    share_recv,
    send_sem,
    recv_sem,
    relay_send,
    relay_recv,
    red_send,
    red_recv,
    pair_sem,
    gather_send,
    gather_recv,
    outer_send,
    outer_recv,
    spread_send,
    spread_recv,
):
    shot = lax.axis_index("shot")
    dom = lax.axis_index("dom")
    column = lax.rem(dom, 4)
    row = dom // 4
    lower = lax.rem(shot // 2, 2)
    eighth = (shot // 4) * 2 + lax.rem(shot, 2)

    def along_dom(step):
        return {"dom": lax.rem(dom + step + GROUP, GROUP)}

    def member(index):
        return {"shot": (index // 2) * 4 + lower * 2 + lax.rem(index, 2)}

    towards = (along_dom(1), along_dom(-1))
    has = (dom < GROUP - 1, dom > 0)
    from_has = (dom > 0, dom < GROUP - 1)
    crosses = (column == 3, column == 0)
    from_crosses = (column == 0, column == 3)
    relays = ((column == 0) & (row < 3), (column == 3) & (row > 0))
    relay_first = (along_dom(-3), along_dom(3))
    relay_second = (along_dom(4), along_dom(-4))

    def load(s):
        return [
            pltpu.make_async_copy(source.at[s], target, load_sem.at[s, k])
            for k, (source, target) in enumerate(
                (
                    (wave_now_hbm, wave0.at[s, pl.ds(1, PLANES)]),
                    (adj_now_hbm, adj0.at[s, pl.ds(1, PLANES)]),
                    (wave_prev_hbm, prev.at[s]),
                    (adj_next_hbm, after.at[s]),
                )
            )
        ]

    small_loads = [
        pltpu.make_async_copy(source, target, small_sem.at[k])
        for k, (source, target) in enumerate(
            (
                (cells_hbm, cells_ref),
                (residual_hbm, residual_ref),
                (vel_hbm, vel),
                (source_cell_hbm, source_cell),
                (source_wave_hbm, source_wave),
                (aperture_hbm, aperture),
            )
        )
    ]
    for copy in small_loads:
        copy.start()
    for s in range(SHOTS):
        for copy in load(s):
            copy.start()

    barrier = pltpu.get_barrier_semaphore()

    def greet(device):
        pl.semaphore_signal(barrier, inc=1, device_id=device, device_id_type=MESH)

    def greet_peer(k, carry):
        greet({"shot": lax.rem(shot + k, GROUP)})
        return carry

    lax.fori_loop(1, GROUP, greet_peer, 0)
    greet(towards[UP])
    greet(towards[DOWN])

    @pl.when(column == 0)
    def _():
        greet(along_dom(3))
        greet(along_dom(4))
        greet(along_dom(-4))

    @pl.when(column == 3)
    def _():
        greet(along_dom(-3))
        greet(along_dom(4))
        greet(along_dom(-4))

    relaying = (column == 0) | (column == 3)
    pl.semaphore_wait(barrier, GROUP + 1 + jnp.where(relaying, 3, 0))

    fields = ((wave_now_hbm, wave0), (adj_now_hbm, adj0), (None, wave1), (None, adj1))

    def layer_refs(k, s, way):
        given, block = fields[k]
        source = ends.at[way, k - 2, s] if given is None else given.at[s, ENDS[way] - 1]
        return source, block.at[s, GHOSTS[way]]

    def remote(source, target, send, recv, device):
        return pltpu.make_async_remote_copy(
            src_ref=source,
            dst_ref=target,
            send_sem=send,
            recv_sem=recv,
            device_id=device,
            device_id_type=MESH,
        )

    first_half, second_half = pl.ds(0, HALF), pl.ds(HALF, HALF)

    def whole(k, s, way):
        source, target = layer_refs(k, s, way)
        return remote(source, target, send_sem.at[way, k, s], recv_sem.at[way, k, s], towards[way])

    def direct(k, s, way):
        source, target = layer_refs(k, s, way)
        return remote(
            source.at[:, first_half],
            target.at[:, first_half],
            send_sem.at[way, k, s],
            recv_sem.at[way, k, s],
            towards[way],
        )

    def leg_one(k, s, way):
        source, _ = layer_refs(k, s, way)
        return remote(
            source.at[:, second_half],
            relay_buf.at[k, s],
            relay_send.at[0, k, s],
            relay_recv.at[0, k, s],
            relay_first[way],
        )

    def leg_two(k, s, way):
        _, target = layer_refs(k, s, way)
        return remote(
            relay_buf.at[k, s],
            target.at[:, second_half],
            relay_send.at[1, k, s],
            relay_recv.at[1, k, s],
            relay_second[way],
        )

    def when_each(conditions, body):
        for way in (UP, DOWN):
            pl.when(conditions[way])(functools.partial(body, way))

    def both(one, other):
        return tuple(a & b for a, b in zip(one, other, strict=True))

    def but(one, other):
        return tuple(a & jnp.logical_not(b) for a, b in zip(one, other, strict=True))

    far, near = both(has, crosses), but(has, crosses)
    from_far, from_near = both(from_has, from_crosses), but(from_has, from_crosses)

    def send_first_legs(k, s):
        when_each(far, lambda way: leg_one(k, s, way).start())

    def send_layer(k, s):
        when_each(far, lambda way: direct(k, s, way).start())
        when_each(near, lambda way: whole(k, s, way).start())

    def advance(k, s):
        when_each(far, lambda way: direct(k, s, way).wait_send())
        when_each(near, lambda way: whole(k, s, way).wait_send())
        pl.when(s < SHOTS - WINDOW)(lambda: send_layer(k, s + WINDOW))
        if k < 3:
            pl.when(s >= SHOTS - WINDOW)(lambda: send_layer(k + 1, s + WINDOW - SHOTS))

        def pass_on(way):
            leg_one(k, s, way).wait_recv()
            leg_two(k, s, way).start()

        when_each(relays, pass_on)

    def take_layer(k, s):
        def two_halves(way):
            direct(k, s, way).wait_recv()
            leg_two(k, s, way).wait_recv()

        when_each(from_far, two_halves)
        when_each(from_near, lambda way: whole(k, s, way).wait_recv())

    def end_legs(k, s):
        when_each(far, lambda way: leg_one(k, s, way).wait_send())
        when_each(relays, lambda way: leg_two(k, s, way).wait_send())

    def eighth_of(index):
        return pl.ds(pl.multiple_of(index * EIGHTH, EIGHTH), EIGHTH)

    def vel_piece(way):
        return remote(
            vel_hbm.at[ENDS[way] - 1, :, eighth_of(eighth)],
            vel_ghost.at[way, :, eighth_of(eighth)],
            vel_send.at[way],
            vel_recv.at[way],
            towards[way],
        )

    def share_vel(k):
        mine = vel_ghost.at[:, :, eighth_of(eighth)]
        peer = member(lax.rem(eighth + k, 8))
        return remote(mine, mine, share_send.at[k], share_recv.at[k], peer)

    def shared_vel(k):
        peer = lax.rem(eighth - k + 8, 8)
        there = vel_ghost.at[:, :, eighth_of(peer)]
        return remote(there, there, share_send.at[k], share_recv.at[k], member(peer))

    eighths = range(1, 8)

    def each_shot(body):
        def step(s, carry):
            body(s)
            return carry

        lax.fori_loop(0, SHOTS, step, 0)

    for k in (0, 1):
        each_shot(functools.partial(send_first_legs, k))
    when_each(has, lambda way: vel_piece(way).start())
    for s in range(WINDOW):
        send_layer(0, s)

    def clear_ghosts(way):
        nothing = jnp.zeros((LEVELS, COLUMNS), jnp.float32)
        vel_ghost[way, :, eighth_of(eighth)] = jnp.zeros((LEVELS, EIGHTH), jnp.float32)

        def clear(s):
            for block in (wave0, adj0, wave1, adj1):
                block[s, GHOSTS[way]] = nothing

        each_shot(clear)

    when_each(tuple(jnp.logical_not(there) for there in from_has), clear_ghosts)

    level = lax.broadcasted_iota(jnp.int32, (LEVELS, LANES), 0)
    lane = lax.broadcasted_iota(jnp.int32, (LEVELS, LANES), 1)
    place = level * LANES + lane
    top, bottom = level == 0, level == LEVELS - 1
    leftmost, rightmost = lane == 0, lane == LANES - 1

    def columns_of(t):
        return pl.ds(t * LANES, LANES)

    def laplace(ref, s, x, sides=None):
        sides = (x - 1, x + 1) if sides is None else sides
        empty = jnp.zeros((LEVELS, LANES), jnp.float32)
        here = ref[s, x, :, columns_of(0)]
        right_of = pltpu.roll(here, LANES - 1, 1)
        before = empty
        for t in range(TILES):
            if t + 1 < TILES:
                following = ref[s, x, :, columns_of(t + 1)]
                right_next = pltpu.roll(following, LANES - 1, 1)
            else:
                following, right_next = empty, empty
            shifted = pltpu.roll(here, 1, 1)
            left = jnp.where(leftmost, before, shifted)
            right = jnp.where(rightmost, right_next, right_of)
            above = jnp.where(top, 0.0, pltpu.roll(here, 1, 0))
            below = jnp.where(bottom, 0.0, pltpu.roll(here, LEVELS - 1, 0))
            beside = (above + below) + (left + right)
            for side in sides:
                beside = beside + ref[s, side, :, columns_of(t)]
            yield here, beside - 6.0 * here
            before, here, right_of = shifted, following, right_next

    def source_of(s):
        local = source_cell[s] - dom * CELLS
        tile = (local >> 14) * TILES + ((local >> 7) & (TILES - 1))
        return (tile * LEVELS + ((local >> 11) & (LEVELS - 1))) * LANES + (local & (LANES - 1))

    def rows_of(x, t):
        return pl.ds(pl.multiple_of(((x - 1) * TILES + t) * LEVELS, LEVELS), LEVELS)

    def first_step(s, x, sides, new_wave, new_adj):
        at = source_of(s) - (x - 1) * (TILES * LEVELS * LANES)
        wavelet = source_wave[0, s]
        pair = zip(laplace(wave0, s, x, sides), laplace(adj0, s, x, sides), strict=True)
        for t, ((wave, wave_lap), (adj, adj_lap)) in enumerate(pair):
            cols = columns_of(t)
            v = vel[x - 1, :, cols]
            pushed = v * wave_lap + jnp.where(place == at - t * (LEVELS * LANES), wavelet, 0.0)
            new_wave[:, cols] = (2.0 * wave - prev[s, x - 1, :, cols]) + pushed
            prev[s, x - 1, :, cols] = pushed
            drawn = injected[s, rows_of(x, t), pl.ds(0, LANES)]
            new_adj[:, cols] = (2.0 * adj - after[s, x - 1, :, cols]) + (v * adj_lap + drawn)

    def second_step(s, x, add):
        at = source_of(s) - (x - 1) * (TILES * LEVELS * LANES)
        wavelet = source_wave[1, s]
        inside = aperture[s, 0] == dom
        for k in range(1, 8):
            inside = inside | (aperture[s, k] == dom)
        weight = jnp.where(inside, scale, 0.0)
        pair = zip(laplace(wave1, s, x), laplace(adj1, s, x), strict=True)
        for t, ((_, wave_lap), (adj, adj_lap)) in enumerate(pair):
            cols = columns_of(t)
            v = vel[x - 1, :, cols]
            pushed = v * wave_lap + jnp.where(place == at - t * (LEVELS * LANES), wavelet, 0.0)
            drawn = injected[s, rows_of(x, t), pl.ds(LANES, LANES)]
            zero = (2.0 * adj - adj0[s, x, :, cols]) + (v * adj_lap + drawn)
            image = weight * (adj * pushed + zero * prev[s, x - 1, :, cols])
            add(t, image)

    def inject(s):
        local = cells_ref[pl.ds(s, 1), :] - dom * CELLS
        tile = (local >> 14) * TILES + ((local >> 7) & (TILES - 1))
        line = tile * LEVELS + ((local >> 11) & (LEVELS - 1))
        spot = local & (LANES - 1)
        lines = PLANES * TILES * LEVELS
        picks = lax.broadcasted_iota(jnp.int32, (lines, RECEIVERS), 0) == line
        picks = jnp.where(picks, 1.0, 0.0).astype(jnp.bfloat16)
        hits = lax.broadcasted_iota(jnp.int32, (LANES, RECEIVERS), 0) == spot
        parts = []
        for step in (0, 1):
            rest = residual_ref[s, pl.ds(step, 1), :]
            pieces = []
            for _ in range(3):
                piece = rest.astype(jnp.bfloat16).astype(jnp.float32)
                rest = rest - piece
                pieces.append(jnp.where(hits, piece, 0.0).astype(jnp.bfloat16))
            parts.append(jnp.concatenate(pieces, axis=1))
        injected[s] = lax.dot_general(
            jnp.concatenate([picks] * 3, axis=1),
            jnp.concatenate(parts, axis=0),
            (((1,), (1,)), ((), ())),
            preferred_element_type=jnp.float32,
        )

    def planes(first, last, body):
        def step(x, carry):
            body(x)
            return carry

        lax.fori_loop(first, last, step, 0)

    def end_plane(way):
        return 1 + (1 - way) * (PLANES - 1)

    def ghost_plane(way):
        return (1 - way) * (PLANES + 1)

    for copy in small_loads:
        copy.wait()

    def phase_one(s):
        advance(0, s)
        inject(s)
        for copy in load(s):
            copy.wait()

        def part(way):
            x = end_plane(way)
            first_step(s, x, (2 + (1 - way) * (PLANES - 3),), ends.at[way, 0, s], ends.at[way, 1, s])

        planes(0, 2, part)
        send_first_legs(2, s)
        send_first_legs(3, s)

    each_shot(phase_one)

    def clear_inner(x):
        inner[x] = jnp.zeros((LEVELS, COLUMNS), jnp.float32)

    def clear_outer(t):
        outer[t] = jnp.zeros((2, LEVELS, LANES), jnp.float32)

    def clear_beside(way):
        beside[way] = jnp.zeros((LEVELS, COLUMNS), jnp.float32)

    planes(0, MIDDLE, clear_inner)
    planes(0, 2, clear_beside)
    planes(0, TILES, clear_outer)
    when_each(from_has, lambda way: vel_piece(way).wait_recv())
    for k in eighths:
        share_vel(k).start()

    def phase_two(s):
        advance(1, s)

        def plane(x):
            first_step(s, x, (x - 1, x + 1), wave1.at[s, x], adj1.at[s, x])

        planes(2, PLANES, plane)

        def middle(x):
            def add(t, image):
                inner[x - 3, :, columns_of(t)] += image

            second_step(s, x, add)

        planes(3, PLANES - 1, middle)

    each_shot(phase_two)

    sets = (
        (inner, inner_got, inner_part, inner_pair, out_ref.at[pl.ds(2, MIDDLE)]),
        (beside, beside_got, beside_part, beside_pair, beside_out),
    )

    def scatter(which, k):
        total, got, _, _, _ = sets[which]
        peer = lax.rem(eighth + k, 8)
        return remote(
            total.at[:, :, eighth_of(peer)],
            got.at[k],
            red_send.at[which, k],
            red_recv.at[which, k],
            member(peer),
        )

    def swap(which):
        _, _, part, pair, _ = sets[which]
        return remote(
            part,
            pair,
            pair_sem.at[which, 0],
            pair_sem.at[which, 1],
            {"shot": shot + 2 - 4 * lower},
        )

    def gather(which, k):
        mine = sets[which][4].at[:, :, eighth_of(eighth)]
        return remote(
            mine,
            mine,
            gather_send.at[which, k],
            gather_recv.at[which, k],
            member(lax.rem(eighth + k, 8)),
        )

    def gathered(which, k):
        peer = lax.rem(eighth - k + 8, 8)
        there = sets[which][4].at[:, :, eighth_of(peer)]
        return remote(
            there, there, gather_send.at[which, k], gather_recv.at[which, k], member(peer)
        )

    def start_sum(which):
        for k in eighths:
            scatter(which, k).start()

    def add_up(which):
        total, got, part, _, _ = sets[which]
        value = total[:, :, eighth_of(eighth)]
        for k in eighths:
            scatter(which, k).wait_recv()
            value = value + got[k]
        part[...] = value
        swap(which).start()

    def give_back(which):
        _, _, part, pair, result = sets[which]
        swap(which).wait_recv()
        result[:, :, eighth_of(eighth)] = part[...] + pair[...]
        for k in eighths:
            gather(which, k).start()

    def end_sum(which):
        swap(which).wait_send()
        for k in eighths:
            scatter(which, k).wait_send()
            gather(which, k).wait_send()
            gathered(which, k).wait_recv()

    def scatter_outer(k):
        peer = lax.rem(shot + k, GROUP)
        return remote(
            outer.at[peer], outer_got.at[k], outer_send.at[k], outer_recv.at[k], {"shot": peer}
        )

    def spread(k):
        mine = outer_out.at[shot]
        return remote(
            mine, mine, spread_send.at[k], spread_recv.at[k], {"shot": lax.rem(shot + k, GROUP)}
        )

    def spread_from(k):
        peer = lax.rem(shot - k + GROUP, GROUP)
        there = outer_out.at[peer]
        return remote(there, there, spread_send.at[k], spread_recv.at[k], {"shot": peer})

    peers = range(1, GROUP)

    def start_outer():
        for k in peers:
            scatter_outer(k).start()

    def sum_outer():
        total = outer[shot]
        for k in peers:
            scatter_outer(k).wait_recv()
            total = total + outer_got[k]
        outer_out[shot] = total
        for k in peers:
            spread(k).start()

    def end_outer():
        for k in peers:
            scatter_outer(k).wait_send()
            spread(k).wait_send()
        for k in peers:
            spread_from(k).wait_recv()
        for t in range(TILES):
            for side in (0, 1):
                out_ref[side * (PLANES - 1), :, columns_of(t)] = outer_out[t, side]

    start_sum(0)

    def phase_three(s):
        advance(2, s)
        take_layer(0, s)
        take_layer(1, s)

        def complete(way):
            x, ghost = end_plane(way), ghost_plane(way)
            v = vel[x - 1]
            pushed = v * wave0[s, ghost]
            wave1[s, x] = ends[way, 0, s] + pushed
            prev[s, x - 1] += pushed
            adj1[s, x] = ends[way, 1, s] + v * adj0[s, ghost]

        planes(0, 2, complete)

        def next_to(way):
            def add(t, image):
                beside[1 - way, :, columns_of(t)] += image

            second_step(s, 2 + (1 - way) * (PLANES - 3), add)

        planes(0, 2, next_to)

    each_shot(phase_three)
    start_sum(1)

    def ends_second(s):
        take_layer(2, s)
        take_layer(3, s)

        def part(way):
            x, ghost = end_plane(way), ghost_plane(way)
            v = vel_ghost[1 - way]
            wave1[s, ghost] += v * wave0[s, x]
            adj1[s, ghost] += v * adj0[s, x]

            def add(t, image):
                outer[t, 1 - way] += image

            second_step(s, x, add)

        planes(0, 2, part)

    advance(3, 0)
    advance(3, 1)
    add_up(0)
    advance(3, 2)
    advance(3, 3)
    give_back(0)
    for k in eighths:
        shared_vel(k).wait_recv()
    add_up(1)

    each_shot(ends_second)
    start_outer()
    give_back(1)
    end_sum(0)
    sum_outer()
    end_sum(1)
    out_ref[1] = beside_out[0]
    out_ref[PLANES - 2] = beside_out[1]

    for k in range(4):
        each_shot(functools.partial(end_legs, k))
    when_each(has, lambda way: vel_piece(way).wait_send())
    for k in eighths:
        share_vel(k).wait_send()
    end_outer()


def body(*arguments):
    arguments = (*arguments[:6], arguments[6].T, *arguments[7:])
    scale = float(lax.axis_size("shot") * SHOTS) ** (-0.5)
    f32 = jnp.float32
    block = (LEVELS, COLUMNS)
    dma = pltpu.SemaphoreType.DMA
    hbm = pl.BlockSpec(memory_space=pltpu.HBM)
    return pl.pallas_call(
        functools.partial(kernel, scale),
        out_shape=pltpu.VMEM((PLANES, *block), f32),
        in_specs=[hbm] * 10,
        out_specs=pl.BlockSpec(memory_space=pltpu.VMEM),
        scratch_shapes=[
            pltpu.SMEM((SHOTS,), jnp.int32),
            pltpu.SMEM((2, SHOTS), f32),
            pltpu.VMEM((SHOTS, RECEIVERS), jnp.int32),
            pltpu.VMEM((SHOTS, 2, RECEIVERS), f32),
            pltpu.SMEM((SHOTS, 8), jnp.int32),
            pltpu.VMEM((PLANES, *block), f32),
            pltpu.VMEM((SHOTS, PLANES + 2, *block), f32),
            pltpu.VMEM((SHOTS, PLANES + 2, *block), f32),
            pltpu.VMEM((SHOTS, PLANES + 2, *block), f32),
            pltpu.VMEM((SHOTS, PLANES + 2, *block), f32),
            pltpu.VMEM((SHOTS, PLANES, *block), f32),
            pltpu.VMEM((SHOTS, PLANES, *block), f32),
            pltpu.VMEM((SHOTS, CELLS // LANES, 2 * LANES), f32),
            pltpu.VMEM((MIDDLE, *block), f32),
            pltpu.VMEM((2, *block), f32),
            pltpu.VMEM((2, *block), f32),
            pltpu.VMEM((TILES, 2, LEVELS, LANES), f32),
            pltpu.VMEM((TILES, 2, LEVELS, LANES), f32),
            pltpu.VMEM((TILES, 2, LEVELS, LANES), f32),
            pltpu.VMEM((2, 2, SHOTS, *block), f32),
            pltpu.VMEM((2, *block), f32),
            pltpu.VMEM((4, SHOTS, LEVELS, HALF), f32),
            pltpu.VMEM((8, MIDDLE, LEVELS, EIGHTH), f32),
            pltpu.VMEM((MIDDLE, LEVELS, EIGHTH), f32),
            pltpu.VMEM((MIDDLE, LEVELS, EIGHTH), f32),
            pltpu.VMEM((8, 2, LEVELS, EIGHTH), f32),
            pltpu.VMEM((2, LEVELS, EIGHTH), f32),
            pltpu.VMEM((2, LEVELS, EIGHTH), f32),
            dma((SHOTS, 4)),
            dma((6,)),
            dma((2,)),
            dma((2,)),
            dma((8,)),
            dma((8,)),
            dma((2, 4, SHOTS)),
            dma((2, 4, SHOTS)),
            dma((2, 4, SHOTS)),
            dma((2, 4, SHOTS)),
            dma((2, 8)),
            dma((2, 8)),
            dma((2, 2)),
            dma((2, 8)),
            dma((2, 8)),
            dma((GROUP,)),
            dma((GROUP,)),
            dma((GROUP,)),
            dma((GROUP,)),
        ],
        compiler_params=pltpu.CompilerParams(
            collective_id=0, has_side_effects=True, vmem_limit_bytes=60 * 2**20
        ),
        name="gradient",
    )(*arguments)


def solution(mesh):
    placed = (
        P("dom", None, None),
        P("shot", "dom", None, None),
        P("shot", "dom", None, None),
        P("shot", "dom", None, None),
        P("shot", "dom", None, None),
        P("shot"),
        P("shot", None),
        P("shot", None),
        P("shot", None, None),
        P("shot", None),
    )
    return jax.shard_map(
        body, mesh=mesh, in_specs=placed, out_specs=P("dom", None, None), check_vma=False
    )
```

```python
import functools

import jax
import jax.numpy as jnp
from jax import lax
from jax.experimental import pallas as pl
from jax.experimental.pallas import tpu as pltpu
from jax.sharding import PartitionSpec as P

MESH = pl.DeviceIdType.MESH
SHOTS = 4
PLANES = 8
LEVELS = 8
COLUMNS = 2048
LANES = 128
TILES = COLUMNS // LANES
RECEIVERS = 256
GROUP = 16
HALF = COLUMNS // 2
CELLS = PLANES * LEVELS * COLUMNS
EIGHTH = COLUMNS // 8
MIDDLE = PLANES - 4
WINDOW = 2
UP, DOWN = 0, 1
ENDS = (PLANES, 1)
GHOSTS = (0, PLANES + 1)


def kernel(
    scale,
    vel_hbm,
    wave_prev_hbm,
    wave_now_hbm,
    adj_next_hbm,
    adj_now_hbm,
    source_cell_hbm,
    source_wave_hbm,
    cells_hbm,
    residual_hbm,
    aperture_hbm,
    out_ref,
    source_cell,
    source_wave,
    cells_ref,
    residual_ref,
    aperture,
    vel,
    wave0,
    wave1,
    adj0,
    adj1,
    prev,
    after,
    injected,
    inner,
    beside,
    beside_out,
    outer,
    outer_got,
    outer_out,
    ends,
    vel_ghost,
    relay_buf,
    inner_got,
    inner_part,
    inner_pair,
    beside_got,
    beside_part,
    beside_pair,
    load_sem,
    small_sem,
    vel_send,
    vel_recv,
    share_send,
    share_recv,
    send_sem,
    recv_sem,
    relay_send,
    relay_recv,
    red_send,
    red_recv,
    pair_sem,
    gather_send,
    gather_recv,
    outer_send,
    outer_recv,
    spread_send,
    spread_recv,
):
    shot = lax.axis_index("shot")
    dom = lax.axis_index("dom")
    column = lax.rem(dom, 4)
    row = dom // 4
    lower = lax.rem(shot // 2, 2)
    eighth = (shot // 4) * 2 + lax.rem(shot, 2)

    def along_dom(step):
        return {"dom": lax.rem(dom + step + GROUP, GROUP)}

    def member(index):
        return {"shot": (index // 2) * 4 + lower * 2 + lax.rem(index, 2)}

    towards = (along_dom(1), along_dom(-1))
    has = (dom < GROUP - 1, dom > 0)
    from_has = (dom > 0, dom < GROUP - 1)
    crosses = (column == 3, column == 0)
    from_crosses = (column == 0, column == 3)
    relays = ((column == 0) & (row < 3), (column == 3) & (row > 0))
    relay_first = (along_dom(-3), along_dom(3))
    relay_second = (along_dom(4), along_dom(-4))

    def load(s):
        return [
            pltpu.make_async_copy(source.at[s], target, load_sem.at[s, k])
            for k, (source, target) in enumerate(
                (
                    (wave_now_hbm, wave0.at[s, pl.ds(1, PLANES)]),
                    (adj_now_hbm, adj0.at[s, pl.ds(1, PLANES)]),
                    (wave_prev_hbm, prev.at[s]),
                    (adj_next_hbm, after.at[s]),
                )
            )
        ]

    small_loads = [
        pltpu.make_async_copy(source, target, small_sem.at[k])
        for k, (source, target) in enumerate(
            (
                (cells_hbm, cells_ref),
                (residual_hbm, residual_ref),
                (vel_hbm, vel),
                (source_cell_hbm, source_cell),
                (source_wave_hbm, source_wave),
                (aperture_hbm, aperture),
            )
        )
    ]
    barrier = pltpu.get_barrier_semaphore()

    def greet(device):
        pl.semaphore_signal(barrier, inc=1, device_id=device, device_id_type=MESH)

    greet(towards[UP])
    greet(towards[DOWN])

    @pl.when(column == 0)
    def _():
        greet(along_dom(3))
        greet(along_dom(4))
        greet(along_dom(-4))

    @pl.when(column == 3)
    def _():
        greet(along_dom(-3))
        greet(along_dom(4))
        greet(along_dom(-4))

    for k in range(1, GROUP):
        greet({"shot": lax.rem(shot + k, GROUP)})

    relaying = (column == 0) | (column == 3)
    pl.semaphore_wait(barrier, GROUP + 1 + jnp.where(relaying, 3, 0))

    fields = ((wave_now_hbm, wave0), (adj_now_hbm, adj0), (None, wave1), (None, adj1))

    def layer_refs(k, s, way):
        given, block = fields[k]
        source = ends.at[way, k - 2, s] if given is None else given.at[s, ENDS[way] - 1]
        return source, block.at[s, GHOSTS[way]]

    def remote(source, target, send, recv, device):
        return pltpu.make_async_remote_copy(
            src_ref=source,
            dst_ref=target,
            send_sem=send,
            recv_sem=recv,
            device_id=device,
            device_id_type=MESH,
        )

    first_half, second_half = pl.ds(0, HALF), pl.ds(HALF, HALF)

    def whole(k, s, way):
        source, target = layer_refs(k, s, way)
        return remote(source, target, send_sem.at[way, k, s], recv_sem.at[way, k, s], towards[way])

    def direct(k, s, way):
        source, target = layer_refs(k, s, way)
        return remote(
            source.at[:, first_half],
            target.at[:, first_half],
            send_sem.at[way, k, s],
            recv_sem.at[way, k, s],
            towards[way],
        )

    def leg_one(k, s, way):
        source, _ = layer_refs(k, s, way)
        return remote(
            source.at[:, second_half],
            relay_buf.at[k, s],
            relay_send.at[0, k, s],
            relay_recv.at[0, k, s],
            relay_first[way],
        )

    def leg_two(k, s, way):
        _, target = layer_refs(k, s, way)
        return remote(
            relay_buf.at[k, s],
            target.at[:, second_half],
            relay_send.at[1, k, s],
            relay_recv.at[1, k, s],
            relay_second[way],
        )

    def when_each(conditions, body):
        for way in (UP, DOWN):
            pl.when(conditions[way])(functools.partial(body, way))

    def both(one, other):
        return tuple(a & b for a, b in zip(one, other, strict=True))

    def but(one, other):
        return tuple(a & jnp.logical_not(b) for a, b in zip(one, other, strict=True))

    far, near = both(has, crosses), but(has, crosses)
    from_far, from_near = both(from_has, from_crosses), but(from_has, from_crosses)

    def send_first_legs(k, s):
        when_each(far, lambda way: leg_one(k, s, way).start())

    def send_layer(k, s):
        when_each(far, lambda way: direct(k, s, way).start())
        when_each(near, lambda way: whole(k, s, way).start())

    def advance(k, s):
        when_each(far, lambda way: direct(k, s, way).wait_send())
        when_each(near, lambda way: whole(k, s, way).wait_send())
        pl.when(s < SHOTS - WINDOW)(lambda: send_layer(k, s + WINDOW))
        if k < 3:
            pl.when(s >= SHOTS - WINDOW)(lambda: send_layer(k + 1, s + WINDOW - SHOTS))

        def pass_on(way):
            leg_one(k, s, way).wait_recv()
            leg_two(k, s, way).start()

        when_each(relays, pass_on)

    def take_layer(k, s):
        def two_halves(way):
            direct(k, s, way).wait_recv()
            leg_two(k, s, way).wait_recv()

        when_each(from_far, two_halves)
        when_each(from_near, lambda way: whole(k, s, way).wait_recv())

    def end_legs(k, s):
        when_each(far, lambda way: leg_one(k, s, way).wait_send())
        when_each(relays, lambda way: leg_two(k, s, way).wait_send())

    def eighth_of(index):
        return pl.ds(pl.multiple_of(index * EIGHTH, EIGHTH), EIGHTH)

    def vel_piece(way):
        return remote(
            vel_hbm.at[ENDS[way] - 1, :, eighth_of(eighth)],
            vel_ghost.at[way, :, eighth_of(eighth)],
            vel_send.at[way],
            vel_recv.at[way],
            towards[way],
        )

    def share_vel(k):
        mine = vel_ghost.at[:, :, eighth_of(eighth)]
        peer = member(lax.rem(eighth + k, 8))
        return remote(mine, mine, share_send.at[k], share_recv.at[k], peer)

    def shared_vel(k):
        peer = lax.rem(eighth - k + 8, 8)
        there = vel_ghost.at[:, :, eighth_of(peer)]
        return remote(there, there, share_send.at[k], share_recv.at[k], member(peer))

    eighths = range(1, 8)

    def each_shot(body):
        def step(s, carry):
            body(s)
            return carry

        lax.fori_loop(0, SHOTS, step, 0)

    for k in (0, 1):
        each_shot(functools.partial(send_first_legs, k))
    when_each(has, lambda way: vel_piece(way).start())
    for s in range(WINDOW):
        send_layer(0, s)

    for copy in small_loads:
        copy.start()
    for s in range(SHOTS):
        for copy in load(s):
            copy.start()

    def clear_ghosts(way):
        nothing = jnp.zeros((LEVELS, COLUMNS), jnp.float32)
        vel_ghost[way, :, eighth_of(eighth)] = jnp.zeros((LEVELS, EIGHTH), jnp.float32)

        def clear(s):
            for block in (wave0, adj0, wave1, adj1):
                block[s, GHOSTS[way]] = nothing

        each_shot(clear)

    when_each(tuple(jnp.logical_not(there) for there in from_has), clear_ghosts)

    level = lax.broadcasted_iota(jnp.int32, (LEVELS, LANES), 0)
    lane = lax.broadcasted_iota(jnp.int32, (LEVELS, LANES), 1)
    place = level * LANES + lane
    top, bottom = level == 0, level == LEVELS - 1
    leftmost, rightmost = lane == 0, lane == LANES - 1

    def columns_of(t):
        return pl.ds(t * LANES, LANES)

    def laplace(ref, s, x, sides=None):
        sides = (x - 1, x + 1) if sides is None else sides
        empty = jnp.zeros((LEVELS, LANES), jnp.float32)
        here = ref[s, x, :, columns_of(0)]
        right_of = pltpu.roll(here, LANES - 1, 1)
        before = empty
        for t in range(TILES):
            if t + 1 < TILES:
                following = ref[s, x, :, columns_of(t + 1)]
                right_next = pltpu.roll(following, LANES - 1, 1)
            else:
                following, right_next = empty, empty
            shifted = pltpu.roll(here, 1, 1)
            left = jnp.where(leftmost, before, shifted)
            right = jnp.where(rightmost, right_next, right_of)
            above = jnp.where(top, 0.0, pltpu.roll(here, 1, 0))
            below = jnp.where(bottom, 0.0, pltpu.roll(here, LEVELS - 1, 0))
            beside = (above + below) + (left + right)
            for side in sides:
                beside = beside + ref[s, side, :, columns_of(t)]
            yield here, beside - 6.0 * here
            before, here, right_of = shifted, following, right_next

    def source_of(s):
        local = source_cell[s] - dom * CELLS
        tile = (local >> 14) * TILES + ((local >> 7) & (TILES - 1))
        return (tile * LEVELS + ((local >> 11) & (LEVELS - 1))) * LANES + (local & (LANES - 1))

    def rows_of(x, t):
        return pl.ds(pl.multiple_of(((x - 1) * TILES + t) * LEVELS, LEVELS), LEVELS)

    def first_step(s, x, sides, new_wave, new_adj):
        at = source_of(s) - (x - 1) * (TILES * LEVELS * LANES)
        wavelet = source_wave[0, s]
        pair = zip(laplace(wave0, s, x, sides), laplace(adj0, s, x, sides), strict=True)
        for t, ((wave, wave_lap), (adj, adj_lap)) in enumerate(pair):
            cols = columns_of(t)
            v = vel[x - 1, :, cols]
            pushed = v * wave_lap + jnp.where(place == at - t * (LEVELS * LANES), wavelet, 0.0)
            new_wave[:, cols] = (2.0 * wave - prev[s, x - 1, :, cols]) + pushed
            prev[s, x - 1, :, cols] = pushed
            drawn = injected[s, rows_of(x, t), pl.ds(0, LANES)]
            new_adj[:, cols] = (2.0 * adj - after[s, x - 1, :, cols]) + (v * adj_lap + drawn)

    def second_step(s, x, add):
        at = source_of(s) - (x - 1) * (TILES * LEVELS * LANES)
        wavelet = source_wave[1, s]
        inside = aperture[s, 0] == dom
        for k in range(1, 8):
            inside = inside | (aperture[s, k] == dom)
        weight = jnp.where(inside, scale, 0.0)
        pair = zip(laplace(wave1, s, x), laplace(adj1, s, x), strict=True)
        for t, ((_, wave_lap), (adj, adj_lap)) in enumerate(pair):
            cols = columns_of(t)
            v = vel[x - 1, :, cols]
            pushed = v * wave_lap + jnp.where(place == at - t * (LEVELS * LANES), wavelet, 0.0)
            drawn = injected[s, rows_of(x, t), pl.ds(LANES, LANES)]
            zero = (2.0 * adj - adj0[s, x, :, cols]) + (v * adj_lap + drawn)
            image = weight * (adj * pushed + zero * prev[s, x - 1, :, cols])
            add(t, image)

    def inject(s):
        local = cells_ref[pl.ds(s, 1), :] - dom * CELLS
        tile = (local >> 14) * TILES + ((local >> 7) & (TILES - 1))
        line = tile * LEVELS + ((local >> 11) & (LEVELS - 1))
        spot = local & (LANES - 1)
        lines = PLANES * TILES * LEVELS
        picks = lax.broadcasted_iota(jnp.int32, (lines, RECEIVERS), 0) == line
        picks = jnp.where(picks, 1.0, 0.0).astype(jnp.bfloat16)
        hits = lax.broadcasted_iota(jnp.int32, (LANES, RECEIVERS), 0) == spot
        parts = []
        for step in (0, 1):
            rest = residual_ref[s, pl.ds(step, 1), :]
            pieces = []
            for _ in range(3):
                piece = rest.astype(jnp.bfloat16).astype(jnp.float32)
                rest = rest - piece
                pieces.append(jnp.where(hits, piece, 0.0).astype(jnp.bfloat16))
            parts.append(jnp.concatenate(pieces, axis=1))
        injected[s] = lax.dot_general(
            jnp.concatenate([picks] * 3, axis=1),
            jnp.concatenate(parts, axis=0),
            (((1,), (1,)), ((), ())),
            preferred_element_type=jnp.float32,
        )

    def planes(first, last, body):
        def step(x, carry):
            body(x)
            return carry

        lax.fori_loop(first, last, step, 0)

    def end_plane(way):
        return 1 + (1 - way) * (PLANES - 1)

    def ghost_plane(way):
        return (1 - way) * (PLANES + 1)

    for copy in small_loads:
        copy.wait()

    def phase_one(s):
        advance(0, s)
        inject(s)
        for copy in load(s):
            copy.wait()

        def part(way):
            x = end_plane(way)
            first_step(s, x, (2 + (1 - way) * (PLANES - 3),), ends.at[way, 0, s], ends.at[way, 1, s])

        planes(0, 2, part)
        send_first_legs(2, s)
        send_first_legs(3, s)

    each_shot(phase_one)

    def clear_inner(x):
        inner[x] = jnp.zeros((LEVELS, COLUMNS), jnp.float32)

    def clear_outer(t):
        outer[t] = jnp.zeros((2, LEVELS, LANES), jnp.float32)

    def clear_beside(way):
        beside[way] = jnp.zeros((LEVELS, COLUMNS), jnp.float32)

    planes(0, MIDDLE, clear_inner)
    planes(0, 2, clear_beside)
    planes(0, TILES, clear_outer)
    when_each(from_has, lambda way: vel_piece(way).wait_recv())
    for k in eighths:
        share_vel(k).start()

    def phase_two(s):
        advance(1, s)

        def plane(x):
            first_step(s, x, (x - 1, x + 1), wave1.at[s, x], adj1.at[s, x])

        planes(2, PLANES, plane)

        def middle(x):
            def add(t, image):
                inner[x - 3, :, columns_of(t)] += image

            second_step(s, x, add)

        planes(3, PLANES - 1, middle)

    each_shot(phase_two)

    sets = (
        (inner, inner_got, inner_part, inner_pair, out_ref.at[pl.ds(2, MIDDLE)]),
        (beside, beside_got, beside_part, beside_pair, beside_out),
    )

    def scatter(which, k):
        total, got, _, _, _ = sets[which]
        peer = lax.rem(eighth + k, 8)
        return remote(
            total.at[:, :, eighth_of(peer)],
            got.at[k],
            red_send.at[which, k],
            red_recv.at[which, k],
            member(peer),
        )

    def swap(which):
        _, _, part, pair, _ = sets[which]
        return remote(
            part,
            pair,
            pair_sem.at[which, 0],
            pair_sem.at[which, 1],
            {"shot": shot + 2 - 4 * lower},
        )

    def gather(which, k):
        mine = sets[which][4].at[:, :, eighth_of(eighth)]
        return remote(
            mine,
            mine,
            gather_send.at[which, k],
            gather_recv.at[which, k],
            member(lax.rem(eighth + k, 8)),
        )

    def gathered(which, k):
        peer = lax.rem(eighth - k + 8, 8)
        there = sets[which][4].at[:, :, eighth_of(peer)]
        return remote(
            there, there, gather_send.at[which, k], gather_recv.at[which, k], member(peer)
        )

    def start_sum(which):
        for k in eighths:
            scatter(which, k).start()

    def add_up(which):
        total, got, part, _, _ = sets[which]
        value = total[:, :, eighth_of(eighth)]
        for k in eighths:
            scatter(which, k).wait_recv()
            value = value + got[k]
        part[...] = value
        swap(which).start()

    def give_back(which):
        _, _, part, pair, result = sets[which]
        swap(which).wait_recv()
        result[:, :, eighth_of(eighth)] = part[...] + pair[...]
        for k in eighths:
            gather(which, k).start()

    def end_sum(which):
        swap(which).wait_send()
        for k in eighths:
            scatter(which, k).wait_send()
            gather(which, k).wait_send()
            gathered(which, k).wait_recv()

    def scatter_outer(k):
        peer = lax.rem(shot + k, GROUP)
        return remote(
            outer.at[peer], outer_got.at[k], outer_send.at[k], outer_recv.at[k], {"shot": peer}
        )

    def spread(k):
        mine = outer_out.at[shot]
        return remote(
            mine, mine, spread_send.at[k], spread_recv.at[k], {"shot": lax.rem(shot + k, GROUP)}
        )

    def spread_from(k):
        peer = lax.rem(shot - k + GROUP, GROUP)
        there = outer_out.at[peer]
        return remote(there, there, spread_send.at[k], spread_recv.at[k], {"shot": peer})

    peers = sorted(range(1, GROUP), key=lambda k: abs(k - GROUP // 2))

    def start_outer():
        for k in peers:
            scatter_outer(k).start()

    def sum_outer():
        total = outer[shot]
        for k in peers:
            scatter_outer(k).wait_recv()
            total = total + outer_got[k]
        outer_out[shot] = total
        for k in peers:
            spread(k).start()

    def end_outer():
        for k in peers:
            scatter_outer(k).wait_send()
            spread(k).wait_send()
        for k in peers:
            spread_from(k).wait_recv()
        for t in range(TILES):
            for side in (0, 1):
                out_ref[side * (PLANES - 1), :, columns_of(t)] = outer_out[t, side]

    start_sum(0)

    def phase_three(s):
        advance(2, s)
        take_layer(0, s)
        take_layer(1, s)

        def complete(way):
            x, ghost = end_plane(way), ghost_plane(way)
            v = vel[x - 1]
            pushed = v * wave0[s, ghost]
            wave1[s, x] = ends[way, 0, s] + pushed
            prev[s, x - 1] += pushed
            adj1[s, x] = ends[way, 1, s] + v * adj0[s, ghost]

        planes(0, 2, complete)

        def next_to(way):
            def add(t, image):
                beside[1 - way, :, columns_of(t)] += image

            second_step(s, 2 + (1 - way) * (PLANES - 3), add)

        planes(0, 2, next_to)

    each_shot(phase_three)
    start_sum(1)

    def ends_second(s):
        take_layer(2, s)
        take_layer(3, s)

        def part(way):
            x, ghost = end_plane(way), ghost_plane(way)
            v = vel_ghost[1 - way]
            wave1[s, ghost] += v * wave0[s, x]
            adj1[s, ghost] += v * adj0[s, x]

            def add(t, image):
                outer[t, 1 - way] += image

            second_step(s, x, add)

        planes(0, 2, part)

    advance(3, 0)
    add_up(0)
    advance(3, 1)
    advance(3, 2)
    advance(3, 3)
    give_back(0)
    for k in eighths:
        shared_vel(k).wait_recv()
    add_up(1)

    each_shot(ends_second)
    start_outer()
    end_sum(0)
    give_back(1)
    sum_outer()
    end_sum(1)
    out_ref[1] = beside_out[0]
    out_ref[PLANES - 2] = beside_out[1]

    for k in range(4):
        each_shot(functools.partial(end_legs, k))
    when_each(has, lambda way: vel_piece(way).wait_send())
    for k in eighths:
        share_vel(k).wait_send()
    end_outer()


def body(*arguments):
    arguments = (*arguments[:6], arguments[6].T, *arguments[7:])
    scale = float(lax.axis_size("shot") * SHOTS) ** (-0.5)
    f32 = jnp.float32
    block = (LEVELS, COLUMNS)
    dma = pltpu.SemaphoreType.DMA
    hbm = pl.BlockSpec(memory_space=pltpu.HBM)
    return pl.pallas_call(
        functools.partial(kernel, scale),
        out_shape=pltpu.VMEM((PLANES, *block), f32),
        in_specs=[hbm] * 10,
        out_specs=pl.BlockSpec(memory_space=pltpu.VMEM),
        scratch_shapes=[
            pltpu.SMEM((SHOTS,), jnp.int32),
            pltpu.SMEM((2, SHOTS), f32),
            pltpu.VMEM((SHOTS, RECEIVERS), jnp.int32),
            pltpu.VMEM((SHOTS, 2, RECEIVERS), f32),
            pltpu.SMEM((SHOTS, 8), jnp.int32),
            pltpu.VMEM((PLANES, *block), f32),
            pltpu.VMEM((SHOTS, PLANES + 2, *block), f32),
            pltpu.VMEM((SHOTS, PLANES + 2, *block), f32),
            pltpu.VMEM((SHOTS, PLANES + 2, *block), f32),
            pltpu.VMEM((SHOTS, PLANES + 2, *block), f32),
            pltpu.VMEM((SHOTS, PLANES, *block), f32),
            pltpu.VMEM((SHOTS, PLANES, *block), f32),
            pltpu.VMEM((SHOTS, CELLS // LANES, 2 * LANES), f32),
            pltpu.VMEM((MIDDLE, *block), f32),
            pltpu.VMEM((2, *block), f32),
            pltpu.VMEM((2, *block), f32),
            pltpu.VMEM((TILES, 2, LEVELS, LANES), f32),
            pltpu.VMEM((TILES, 2, LEVELS, LANES), f32),
            pltpu.VMEM((TILES, 2, LEVELS, LANES), f32),
            pltpu.VMEM((2, 2, SHOTS, *block), f32),
            pltpu.VMEM((2, *block), f32),
            pltpu.VMEM((4, SHOTS, LEVELS, HALF), f32),
            pltpu.VMEM((8, MIDDLE, LEVELS, EIGHTH), f32),
            pltpu.VMEM((MIDDLE, LEVELS, EIGHTH), f32),
            pltpu.VMEM((MIDDLE, LEVELS, EIGHTH), f32),
            pltpu.VMEM((8, 2, LEVELS, EIGHTH), f32),
            pltpu.VMEM((2, LEVELS, EIGHTH), f32),
            pltpu.VMEM((2, LEVELS, EIGHTH), f32),
            dma((SHOTS, 4)),
            dma((6,)),
            dma((2,)),
            dma((2,)),
            dma((8,)),
            dma((8,)),
            dma((2, 4, SHOTS)),
            dma((2, 4, SHOTS)),
            dma((2, 4, SHOTS)),
            dma((2, 4, SHOTS)),
            dma((2, 8)),
            dma((2, 8)),
            dma((2, 2)),
            dma((2, 8)),
            dma((2, 8)),
            dma((GROUP,)),
            dma((GROUP,)),
            dma((GROUP,)),
            dma((GROUP,)),
        ],
        compiler_params=pltpu.CompilerParams(
            collective_id=0, has_side_effects=True, vmem_limit_bytes=60 * 2**20
        ),
        name="gradient",
    )(*arguments)


def solution(mesh):
    placed = (
        P("dom", None, None),
        P("shot", "dom", None, None),
        P("shot", "dom", None, None),
        P("shot", "dom", None, None),
        P("shot", "dom", None, None),
        P("shot"),
        P("shot", None),
        P("shot", None),
        P("shot", None, None),
        P("shot", None),
    )
    return jax.shard_map(
        body, mesh=mesh, in_specs=placed, out_specs=P("dom", None, None), check_vma=False
    )
```

```python
import functools

import jax
import jax.numpy as jnp
from jax import lax
from jax.experimental import pallas as pl
from jax.experimental.pallas import tpu as pltpu
from jax.sharding import PartitionSpec as P

MESH = pl.DeviceIdType.MESH
SHOTS = 4
PLANES = 8
LEVELS = 8
COLUMNS = 2048
LANES = 128
TILES = COLUMNS // LANES
RECEIVERS = 256
GROUP = 16
HALF = COLUMNS // 2
CELLS = PLANES * LEVELS * COLUMNS
EIGHTH = COLUMNS // 8
MIDDLE = PLANES - 4
WINDOW = 2
UP, DOWN = 0, 1
ENDS = (PLANES, 1)
GHOSTS = (0, PLANES + 1)


def kernel(
    scale,
    vel_hbm,
    wave_prev_hbm,
    wave_now_hbm,
    adj_next_hbm,
    adj_now_hbm,
    source_cell_hbm,
    source_wave_hbm,
    cells_hbm,
    residual_hbm,
    aperture_hbm,
    out_ref,
    source_cell,
    source_wave,
    cells_ref,
    residual_ref,
    aperture,
    vel,
    wave0,
    wave1,
    adj0,
    adj1,
    prev,
    after,
    injected,
    inner,
    beside,
    beside_out,
    outer,
    outer_got,
    outer_out,
    ends,
    vel_ghost,
    relay_buf,
    inner_got,
    inner_part,
    inner_pair,
    beside_got,
    beside_part,
    beside_pair,
    load_sem,
    small_sem,
    vel_send,
    vel_recv,
    share_send,
    share_recv,
    send_sem,
    recv_sem,
    relay_send,
    relay_recv,
    red_send,
    red_recv,
    pair_sem,
    gather_send,
    gather_recv,
    outer_send,
    outer_recv,
    spread_send,
    spread_recv,
):
    shot = lax.axis_index("shot")
    dom = lax.axis_index("dom")
    column = lax.rem(dom, 4)
    row = dom // 4
    lower = lax.rem(shot // 2, 2)
    eighth = (shot // 4) * 2 + lax.rem(shot, 2)

    def along_dom(step):
        return {"dom": lax.rem(dom + step + GROUP, GROUP)}

    def member(index):
        return {"shot": (index // 2) * 4 + lower * 2 + lax.rem(index, 2)}

    towards = (along_dom(1), along_dom(-1))
    has = (dom < GROUP - 1, dom > 0)
    from_has = (dom > 0, dom < GROUP - 1)
    crosses = (column == 3, column == 0)
    from_crosses = (column == 0, column == 3)
    relays = ((column == 0) & (row < 3), (column == 3) & (row > 0))
    relay_first = (along_dom(-3), along_dom(3))
    relay_second = (along_dom(4), along_dom(-4))

    def load(s):
        return [
            pltpu.make_async_copy(source.at[s], target, load_sem.at[s, k])
            for k, (source, target) in enumerate(
                (
                    (wave_now_hbm, wave0.at[s, pl.ds(1, PLANES)]),
                    (adj_now_hbm, adj0.at[s, pl.ds(1, PLANES)]),
                    (wave_prev_hbm, prev.at[s]),
                    (adj_next_hbm, after.at[s]),
                )
            )
        ]

    small_loads = [
        pltpu.make_async_copy(source, target, small_sem.at[k])
        for k, (source, target) in enumerate(
            (
                (cells_hbm, cells_ref),
                (residual_hbm, residual_ref),
                (vel_hbm, vel),
                (source_cell_hbm, source_cell),
                (source_wave_hbm, source_wave),
                (aperture_hbm, aperture),
            )
        )
    ]
    barrier = pltpu.get_barrier_semaphore()

    def greet(device):
        pl.semaphore_signal(barrier, inc=1, device_id=device, device_id_type=MESH)

    greet(towards[UP])
    greet(towards[DOWN])

    @pl.when(column == 0)
    def _():
        greet(along_dom(3))
        greet(along_dom(4))
        greet(along_dom(-4))

    @pl.when(column == 3)
    def _():
        greet(along_dom(-3))
        greet(along_dom(4))
        greet(along_dom(-4))

    for k in range(1, GROUP):
        greet({"shot": lax.rem(shot + k, GROUP)})

    relaying = (column == 0) | (column == 3)
    pl.semaphore_wait(barrier, GROUP + 1 + jnp.where(relaying, 3, 0))

    fields = ((wave_now_hbm, wave0), (adj_now_hbm, adj0), (None, wave1), (None, adj1))

    def layer_refs(k, s, way):
        given, block = fields[k]
        source = ends.at[way, k - 2, s] if given is None else given.at[s, ENDS[way] - 1]
        return source, block.at[s, GHOSTS[way]]

    def remote(source, target, send, recv, device):
        return pltpu.make_async_remote_copy(
            src_ref=source,
            dst_ref=target,
            send_sem=send,
            recv_sem=recv,
            device_id=device,
            device_id_type=MESH,
        )

    first_half, second_half = pl.ds(0, HALF), pl.ds(HALF, HALF)

    def whole(k, s, way):
        source, target = layer_refs(k, s, way)
        return remote(source, target, send_sem.at[way, k, s], recv_sem.at[way, k, s], towards[way])

    def direct(k, s, way):
        source, target = layer_refs(k, s, way)
        return remote(
            source.at[:, first_half],
            target.at[:, first_half],
            send_sem.at[way, k, s],
            recv_sem.at[way, k, s],
            towards[way],
        )

    def leg_one(k, s, way):
        source, _ = layer_refs(k, s, way)
        return remote(
            source.at[:, second_half],
            relay_buf.at[k, s],
            relay_send.at[0, k, s],
            relay_recv.at[0, k, s],
            relay_first[way],
        )

    def leg_two(k, s, way):
        _, target = layer_refs(k, s, way)
        return remote(
            relay_buf.at[k, s],
            target.at[:, second_half],
            relay_send.at[1, k, s],
            relay_recv.at[1, k, s],
            relay_second[way],
        )

    def when_each(conditions, body):
        for way in (UP, DOWN):
            pl.when(conditions[way])(functools.partial(body, way))

    def both(one, other):
        return tuple(a & b for a, b in zip(one, other, strict=True))

    def but(one, other):
        return tuple(a & jnp.logical_not(b) for a, b in zip(one, other, strict=True))

    far, near = both(has, crosses), but(has, crosses)
    from_far, from_near = both(from_has, from_crosses), but(from_has, from_crosses)

    def send_first_legs(k, s):
        when_each(far, lambda way: leg_one(k, s, way).start())

    def send_layer(k, s):
        when_each(far, lambda way: direct(k, s, way).start())
        when_each(near, lambda way: whole(k, s, way).start())

    def advance(k, s):
        when_each(far, lambda way: direct(k, s, way).wait_send())
        when_each(near, lambda way: whole(k, s, way).wait_send())
        pl.when(s < SHOTS - WINDOW)(lambda: send_layer(k, s + WINDOW))
        if k < 3:
            pl.when(s >= SHOTS - WINDOW)(lambda: send_layer(k + 1, s + WINDOW - SHOTS))

        def pass_on(way):
            leg_one(k, s, way).wait_recv()
            leg_two(k, s, way).start()

        when_each(relays, pass_on)

    def take_layer(k, s):
        def two_halves(way):
            direct(k, s, way).wait_recv()
            leg_two(k, s, way).wait_recv()

        when_each(from_far, two_halves)
        when_each(from_near, lambda way: whole(k, s, way).wait_recv())

    def end_legs(k, s):
        when_each(far, lambda way: leg_one(k, s, way).wait_send())
        when_each(relays, lambda way: leg_two(k, s, way).wait_send())

    def eighth_of(index):
        return pl.ds(pl.multiple_of(index * EIGHTH, EIGHTH), EIGHTH)

    def vel_piece(way):
        return remote(
            vel_hbm.at[ENDS[way] - 1, :, eighth_of(eighth)],
            vel_ghost.at[way, :, eighth_of(eighth)],
            vel_send.at[way],
            vel_recv.at[way],
            towards[way],
        )

    def share_vel(k):
        mine = vel_ghost.at[:, :, eighth_of(eighth)]
        peer = member(lax.rem(eighth + k, 8))
        return remote(mine, mine, share_send.at[k], share_recv.at[k], peer)

    def shared_vel(k):
        peer = lax.rem(eighth - k + 8, 8)
        there = vel_ghost.at[:, :, eighth_of(peer)]
        return remote(there, there, share_send.at[k], share_recv.at[k], member(peer))

    eighths = sorted(range(1, 8), key=lambda k: abs(k - 4))

    def each_shot(body):
        def step(s, carry):
            body(s)
            return carry

        lax.fori_loop(0, SHOTS, step, 0)

    for k in (0, 1):
        each_shot(functools.partial(send_first_legs, k))
    when_each(has, lambda way: vel_piece(way).start())
    for s in range(WINDOW):
        send_layer(0, s)

    for copy in small_loads:
        copy.start()
    for s in range(SHOTS):
        for copy in load(s):
            copy.start()

    def clear_ghosts(way):
        nothing = jnp.zeros((LEVELS, COLUMNS), jnp.float32)
        vel_ghost[way, :, eighth_of(eighth)] = jnp.zeros((LEVELS, EIGHTH), jnp.float32)

        def clear(s):
            for block in (wave0, adj0, wave1, adj1):
                block[s, GHOSTS[way]] = nothing

        each_shot(clear)

    when_each(tuple(jnp.logical_not(there) for there in from_has), clear_ghosts)

    level = lax.broadcasted_iota(jnp.int32, (LEVELS, LANES), 0)
    lane = lax.broadcasted_iota(jnp.int32, (LEVELS, LANES), 1)
    place = level * LANES + lane
    top, bottom = level == 0, level == LEVELS - 1
    leftmost, rightmost = lane == 0, lane == LANES - 1

    def columns_of(t):
        return pl.ds(t * LANES, LANES)

    def laplace(ref, s, x, sides=None):
        sides = (x - 1, x + 1) if sides is None else sides
        empty = jnp.zeros((LEVELS, LANES), jnp.float32)
        here = ref[s, x, :, columns_of(0)]
        right_of = pltpu.roll(here, LANES - 1, 1)
        before = empty
        for t in range(TILES):
            if t + 1 < TILES:
                following = ref[s, x, :, columns_of(t + 1)]
                right_next = pltpu.roll(following, LANES - 1, 1)
            else:
                following, right_next = empty, empty
            shifted = pltpu.roll(here, 1, 1)
            left = jnp.where(leftmost, before, shifted)
            right = jnp.where(rightmost, right_next, right_of)
            above = jnp.where(top, 0.0, pltpu.roll(here, 1, 0))
            below = jnp.where(bottom, 0.0, pltpu.roll(here, LEVELS - 1, 0))
            beside = (above + below) + (left + right)
            for side in sides:
                beside = beside + ref[s, side, :, columns_of(t)]
            yield here, beside - 6.0 * here
            before, here, right_of = shifted, following, right_next

    def source_of(s):
        local = source_cell[s] - dom * CELLS
        tile = (local >> 14) * TILES + ((local >> 7) & (TILES - 1))
        return (tile * LEVELS + ((local >> 11) & (LEVELS - 1))) * LANES + (local & (LANES - 1))

    def rows_of(x, t):
        return pl.ds(pl.multiple_of(((x - 1) * TILES + t) * LEVELS, LEVELS), LEVELS)

    def first_step(s, x, sides, new_wave, new_adj):
        at = source_of(s) - (x - 1) * (TILES * LEVELS * LANES)
        wavelet = source_wave[0, s]
        pair = zip(laplace(wave0, s, x, sides), laplace(adj0, s, x, sides), strict=True)
        for t, ((wave, wave_lap), (adj, adj_lap)) in enumerate(pair):
            cols = columns_of(t)
            v = vel[x - 1, :, cols]
            pushed = v * wave_lap + jnp.where(place == at - t * (LEVELS * LANES), wavelet, 0.0)
            new_wave[:, cols] = (2.0 * wave - prev[s, x - 1, :, cols]) + pushed
            prev[s, x - 1, :, cols] = pushed
            drawn = injected[s, rows_of(x, t), pl.ds(0, LANES)]
            new_adj[:, cols] = (2.0 * adj - after[s, x - 1, :, cols]) + (v * adj_lap + drawn)

    def second_step(s, x, add):
        at = source_of(s) - (x - 1) * (TILES * LEVELS * LANES)
        wavelet = source_wave[1, s]
        inside = aperture[s, 0] == dom
        for k in range(1, 8):
            inside = inside | (aperture[s, k] == dom)
        weight = jnp.where(inside, scale, 0.0)
        pair = zip(laplace(wave1, s, x), laplace(adj1, s, x), strict=True)
        for t, ((_, wave_lap), (adj, adj_lap)) in enumerate(pair):
            cols = columns_of(t)
            v = vel[x - 1, :, cols]
            pushed = v * wave_lap + jnp.where(place == at - t * (LEVELS * LANES), wavelet, 0.0)
            drawn = injected[s, rows_of(x, t), pl.ds(LANES, LANES)]
            zero = (2.0 * adj - adj0[s, x, :, cols]) + (v * adj_lap + drawn)
            image = weight * (adj * pushed + zero * prev[s, x - 1, :, cols])
            add(t, image)

    def inject(s):
        local = cells_ref[pl.ds(s, 1), :] - dom * CELLS
        tile = (local >> 14) * TILES + ((local >> 7) & (TILES - 1))
        line = tile * LEVELS + ((local >> 11) & (LEVELS - 1))
        spot = local & (LANES - 1)
        lines = PLANES * TILES * LEVELS
        picks = lax.broadcasted_iota(jnp.int32, (lines, RECEIVERS), 0) == line
        picks = jnp.where(picks, 1.0, 0.0).astype(jnp.bfloat16)
        hits = lax.broadcasted_iota(jnp.int32, (LANES, RECEIVERS), 0) == spot
        parts = []
        for step in (0, 1):
            rest = residual_ref[s, pl.ds(step, 1), :]
            pieces = []
            for _ in range(3):
                piece = rest.astype(jnp.bfloat16).astype(jnp.float32)
                rest = rest - piece
                pieces.append(jnp.where(hits, piece, 0.0).astype(jnp.bfloat16))
            parts.append(jnp.concatenate(pieces, axis=1))
        injected[s] = lax.dot_general(
            jnp.concatenate([picks] * 3, axis=1),
            jnp.concatenate(parts, axis=0),
            (((1,), (1,)), ((), ())),
            preferred_element_type=jnp.float32,
        )

    def planes(first, last, body):
        def step(x, carry):
            body(x)
            return carry

        lax.fori_loop(first, last, step, 0)

    def end_plane(way):
        return 1 + (1 - way) * (PLANES - 1)

    def ghost_plane(way):
        return (1 - way) * (PLANES + 1)

    for copy in small_loads:
        copy.wait()

    def phase_one(s):
        advance(0, s)
        inject(s)
        for copy in load(s):
            copy.wait()

        def part(way):
            x = end_plane(way)
            first_step(s, x, (2 + (1 - way) * (PLANES - 3),), ends.at[way, 0, s], ends.at[way, 1, s])

        planes(0, 2, part)
        send_first_legs(2, s)
        send_first_legs(3, s)

    each_shot(phase_one)

    def clear_inner(x):
        inner[x] = jnp.zeros((LEVELS, COLUMNS), jnp.float32)

    def clear_outer(t):
        outer[t] = jnp.zeros((2, LEVELS, LANES), jnp.float32)

    def clear_beside(way):
        beside[way] = jnp.zeros((LEVELS, COLUMNS), jnp.float32)

    planes(0, MIDDLE, clear_inner)
    planes(0, 2, clear_beside)
    planes(0, TILES, clear_outer)
    when_each(from_has, lambda way: vel_piece(way).wait_recv())
    for k in eighths:
        share_vel(k).start()

    def phase_two(s):
        advance(1, s)

        def plane(x):
            first_step(s, x, (x - 1, x + 1), wave1.at[s, x], adj1.at[s, x])

        planes(2, PLANES, plane)

        def middle(x):
            def add(t, image):
                inner[x - 3, :, columns_of(t)] += image

            second_step(s, x, add)

        planes(3, PLANES - 1, middle)

    each_shot(phase_two)

    sets = (
        (inner, inner_got, inner_part, inner_pair, out_ref.at[pl.ds(2, MIDDLE)]),
        (beside, beside_got, beside_part, beside_pair, beside_out),
    )

    def scatter(which, k):
        total, got, _, _, _ = sets[which]
        peer = lax.rem(eighth + k, 8)
        return remote(
            total.at[:, :, eighth_of(peer)],
            got.at[k],
            red_send.at[which, k],
            red_recv.at[which, k],
            member(peer),
        )

    def swap(which):
        _, _, part, pair, _ = sets[which]
        return remote(
            part,
            pair,
            pair_sem.at[which, 0],
            pair_sem.at[which, 1],
            {"shot": shot + 2 - 4 * lower},
        )

    def gather(which, k):
        mine = sets[which][4].at[:, :, eighth_of(eighth)]
        return remote(
            mine,
            mine,
            gather_send.at[which, k],
            gather_recv.at[which, k],
            member(lax.rem(eighth + k, 8)),
        )

    def gathered(which, k):
        peer = lax.rem(eighth - k + 8, 8)
        there = sets[which][4].at[:, :, eighth_of(peer)]
        return remote(
            there, there, gather_send.at[which, k], gather_recv.at[which, k], member(peer)
        )

    def start_sum(which):
        for k in eighths:
            scatter(which, k).start()

    def add_up(which):
        total, got, part, _, _ = sets[which]
        value = total[:, :, eighth_of(eighth)]
        for k in eighths:
            scatter(which, k).wait_recv()
            value = value + got[k]
        part[...] = value
        swap(which).start()

    def give_back(which):
        _, _, part, pair, result = sets[which]
        swap(which).wait_recv()
        result[:, :, eighth_of(eighth)] = part[...] + pair[...]
        for k in eighths:
            gather(which, k).start()

    def end_sum(which):
        swap(which).wait_send()
        for k in eighths:
            scatter(which, k).wait_send()
            gather(which, k).wait_send()
            gathered(which, k).wait_recv()

    def scatter_outer(k):
        peer = lax.rem(shot + k, GROUP)
        return remote(
            outer.at[peer], outer_got.at[k], outer_send.at[k], outer_recv.at[k], {"shot": peer}
        )

    def spread(k):
        mine = outer_out.at[shot]
        return remote(
            mine, mine, spread_send.at[k], spread_recv.at[k], {"shot": lax.rem(shot + k, GROUP)}
        )

    def spread_from(k):
        peer = lax.rem(shot - k + GROUP, GROUP)
        there = outer_out.at[peer]
        return remote(there, there, spread_send.at[k], spread_recv.at[k], {"shot": peer})

    peers = sorted(range(1, GROUP), key=lambda k: abs(k - GROUP // 2))

    def start_outer():
        for k in peers:
            scatter_outer(k).start()

    def sum_outer():
        total = outer[shot]
        for k in peers:
            scatter_outer(k).wait_recv()
            total = total + outer_got[k]
        outer_out[shot] = total
        for k in peers:
            spread(k).start()

    def end_outer():
        for k in peers:
            scatter_outer(k).wait_send()
            spread(k).wait_send()
        for k in peers:
            spread_from(k).wait_recv()
        for t in range(TILES):
            for side in (0, 1):
                out_ref[side * (PLANES - 1), :, columns_of(t)] = outer_out[t, side]

    start_sum(0)

    def phase_three(s):
        advance(2, s)
        take_layer(0, s)
        take_layer(1, s)

        def complete(way):
            x, ghost = end_plane(way), ghost_plane(way)
            v = vel[x - 1]
            pushed = v * wave0[s, ghost]
            wave1[s, x] = ends[way, 0, s] + pushed
            prev[s, x - 1] += pushed
            adj1[s, x] = ends[way, 1, s] + v * adj0[s, ghost]

        planes(0, 2, complete)

        def next_to(way):
            def add(t, image):
                beside[1 - way, :, columns_of(t)] += image

            second_step(s, 2 + (1 - way) * (PLANES - 3), add)

        planes(0, 2, next_to)

    each_shot(phase_three)
    start_sum(1)

    def ends_second(s):
        take_layer(2, s)
        take_layer(3, s)

        def part(way):
            x, ghost = end_plane(way), ghost_plane(way)
            v = vel_ghost[1 - way]
            wave1[s, ghost] += v * wave0[s, x]
            adj1[s, ghost] += v * adj0[s, x]

            def add(t, image):
                outer[t, 1 - way] += image

            second_step(s, x, add)

        planes(0, 2, part)

    advance(3, 0)
    add_up(0)
    advance(3, 1)
    advance(3, 2)
    advance(3, 3)
    give_back(0)
    for k in eighths:
        shared_vel(k).wait_recv()
    add_up(1)

    each_shot(ends_second)
    start_outer()
    end_sum(0)
    give_back(1)
    sum_outer()
    end_sum(1)
    out_ref[1] = beside_out[0]
    out_ref[PLANES - 2] = beside_out[1]

    for k in range(4):
        each_shot(functools.partial(end_legs, k))
    when_each(has, lambda way: vel_piece(way).wait_send())
    for k in eighths:
        share_vel(k).wait_send()
    end_outer()


def body(*arguments):
    arguments = (*arguments[:6], arguments[6].T, *arguments[7:])
    scale = float(lax.axis_size("shot") * SHOTS) ** (-0.5)
    f32 = jnp.float32
    block = (LEVELS, COLUMNS)
    dma = pltpu.SemaphoreType.DMA
    hbm = pl.BlockSpec(memory_space=pltpu.HBM)
    return pl.pallas_call(
        functools.partial(kernel, scale),
        out_shape=pltpu.VMEM((PLANES, *block), f32),
        in_specs=[hbm] * 10,
        out_specs=pl.BlockSpec(memory_space=pltpu.VMEM),
        scratch_shapes=[
            pltpu.SMEM((SHOTS,), jnp.int32),
            pltpu.SMEM((2, SHOTS), f32),
            pltpu.VMEM((SHOTS, RECEIVERS), jnp.int32),
            pltpu.VMEM((SHOTS, 2, RECEIVERS), f32),
            pltpu.SMEM((SHOTS, 8), jnp.int32),
            pltpu.VMEM((PLANES, *block), f32),
            pltpu.VMEM((SHOTS, PLANES + 2, *block), f32),
            pltpu.VMEM((SHOTS, PLANES + 2, *block), f32),
            pltpu.VMEM((SHOTS, PLANES + 2, *block), f32),
            pltpu.VMEM((SHOTS, PLANES + 2, *block), f32),
            pltpu.VMEM((SHOTS, PLANES, *block), f32),
            pltpu.VMEM((SHOTS, PLANES, *block), f32),
            pltpu.VMEM((SHOTS, CELLS // LANES, 2 * LANES), f32),
            pltpu.VMEM((MIDDLE, *block), f32),
            pltpu.VMEM((2, *block), f32),
            pltpu.VMEM((2, *block), f32),
            pltpu.VMEM((TILES, 2, LEVELS, LANES), f32),
            pltpu.VMEM((TILES, 2, LEVELS, LANES), f32),
            pltpu.VMEM((TILES, 2, LEVELS, LANES), f32),
            pltpu.VMEM((2, 2, SHOTS, *block), f32),
            pltpu.VMEM((2, *block), f32),
            pltpu.VMEM((4, SHOTS, LEVELS, HALF), f32),
            pltpu.VMEM((8, MIDDLE, LEVELS, EIGHTH), f32),
            pltpu.VMEM((MIDDLE, LEVELS, EIGHTH), f32),
            pltpu.VMEM((MIDDLE, LEVELS, EIGHTH), f32),
            pltpu.VMEM((8, 2, LEVELS, EIGHTH), f32),
            pltpu.VMEM((2, LEVELS, EIGHTH), f32),
            pltpu.VMEM((2, LEVELS, EIGHTH), f32),
            dma((SHOTS, 4)),
            dma((6,)),
            dma((2,)),
            dma((2,)),
            dma((8,)),
            dma((8,)),
            dma((2, 4, SHOTS)),
            dma((2, 4, SHOTS)),
            dma((2, 4, SHOTS)),
            dma((2, 4, SHOTS)),
            dma((2, 8)),
            dma((2, 8)),
            dma((2, 2)),
            dma((2, 8)),
            dma((2, 8)),
            dma((GROUP,)),
            dma((GROUP,)),
            dma((GROUP,)),
            dma((GROUP,)),
        ],
        compiler_params=pltpu.CompilerParams(
            collective_id=0, has_side_effects=True, vmem_limit_bytes=60 * 2**20
        ),
        name="gradient",
    )(*arguments)


def solution(mesh):
    placed = (
        P("dom", None, None),
        P("shot", "dom", None, None),
        P("shot", "dom", None, None),
        P("shot", "dom", None, None),
        P("shot", "dom", None, None),
        P("shot"),
        P("shot", None),
        P("shot", None),
        P("shot", None, None),
        P("shot", None),
    )
    return jax.shard_map(
        body, mesh=mesh, in_specs=placed, out_specs=P("dom", None, None), check_vma=False
    )
```
